256 devices in a mesh: dp: 2 (over y_hi), row: 8 (over z), col: 16 (over x, y_lo, core).
Axes of the slice: x: 4, y: 4 (y_hi: 2, y_lo: 2; y = y_hi * 2 + y_lo), z: 8, core: 2. Of those that a mesh axis runs over, the one named last changes fastest.
Arguments:
- out_grads: bfloat16 [512, 28672], P('row', ('dp', 'col')), may hold values from -6 to 6
- layer_inputs: bfloat16 [512, 8192], P('col', ('dp', 'row')), may hold values from -6 to 6
- basis_output: bfloat16 [28672, 28672], P(('dp', 'col'), 'row'), may hold values from -0.03125 to 0.03125
- basis_input: bfloat16 [8192, 8192], P(('dp', 'row'), 'col'), may hold values from -0.0625 to 0.0625
- eigenvalues: bfloat16 [28672, 8192], P('row', 'col'), may hold values from 0.0009 to 405
- query_left: bfloat16 [28672, 128], P(('dp', 'col')), may hold values from -0.03125 to 0.03125
- query_right: bfloat16 [8192, 128], P(('dp', 'row')), may hold values from -0.01171875 to 0.01171875
Outputs:
- influence: float32 [4, 512], P('dp')
The draws below stay inside these ranges and needn't reach their ends.
All inputs are finite; a program needn't handle non-finite values.
Results may differ from the reference program's by a relative error of at most 0.005.
Values may be sent and summed in bfloat16 or wider, within the bound.
A program may use at most 64 MiB of HBM per device.

```python
import math
import jax
import jax.numpy as jnp
from jax import lax

DG = 28672
DA = 8192
RANK = 32
NQ = 4
TOK = 512
N_ROW = 8


def draw_eigenvalues(key, part):
    row_key, column_key, cell_key = jax.random.split(key, 3)
    row_share = jnp.arange(DG, dtype=jnp.float32) / max(DG - 1, 1)
    column_share = jnp.arange(DA, dtype=jnp.float32) / max(DA - 1, 1)
    trend_rate = math.log(3.0)
    cell_factor = 0.1 * jnp.exp(math.log(10.0) * jax.random.uniform(cell_key, (DG, DA), jnp.float32))
    row_scale = jnp.exp(math.log(10.0) * jax.random.uniform(row_key, (DG,), jnp.float32) + trend_rate * row_share)
    column_scale = jnp.exp(math.log(10.0) * jax.random.uniform(column_key, (DA,), jnp.float32) + trend_rate * column_share)
    values = 0.05 * row_scale[:, None] * column_scale[None, :] * cell_factor
    return values.astype(jnp.bfloat16)


def level_of(key, dims, pieces, low, largest):
    loudness = 1.0
    for dim, blocks in pieces:
        draws = jax.random.uniform(jax.random.fold_in(jax.random.fold_in(key, 6), dim), (blocks,), jnp.float32, low / len(pieces), largest / len(pieces))
        loudness = loudness * jnp.repeat(jnp.exp(draws), dims[dim] // blocks).reshape((-1,) + (1,) * (len(dims) - 1 - dim))
    return loudness


def bell_draw(own_key, shape, width, reach, pieces=(), kind=jnp.bfloat16):
    level = level_of(own_key, shape, pieces, -0.22, 0.18) if pieces else 1.0
    values = jax.random.normal(own_key, shape, jnp.float32) * width * level
    return jnp.minimum(jnp.maximum(values, -reach), reach).astype(kind)


def setup_inputs(seed: int = 0) -> dict:
    streams_of = jax.random.split(jax.random.key(seed), 8)
    out_grads = bell_draw(streams_of[0], (TOK, DG), 1.0, 6.0, ((0, 8), (1, 32)))
    layer_inputs = bell_draw(streams_of[1], (TOK, DA), 1.0, 6.0, ((0, 16), (1, 16)))
    basis_output = bell_draw(streams_of[2], (DG, DG), DG ** -0.5, 0.03125, ((0, 32), (1, 8)))
    basis_input = bell_draw(streams_of[3], (DA, DA), DA ** -0.5, 0.0625, ((0, 16), (1, 16)))
    eigenvalues = draw_eigenvalues(jax.random.fold_in(streams_of[7], 71), 0)
    query_left = bell_draw(streams_of[5], (DG, NQ * RANK), DG ** -0.5, 0.03125, ((0, 32),))
    query_right = bell_draw(streams_of[6], (DA, NQ * RANK), (DA * RANK) ** -0.5, 0.01171875, ((0, 16),))
    return {"out_grads": out_grads, "layer_inputs": layer_inputs, "basis_output": basis_output, "basis_input": basis_input, "eigenvalues": eigenvalues, "query_left": query_left, "query_right": query_right}


DAMP_RATIO = 0.1


def reference(out_grads, layer_inputs, basis_output, basis_input, eigenvalues, query_left, query_right):
    rotated_grads = jnp.dot(out_grads, basis_output, preferred_element_type=jnp.float32).astype(jnp.bfloat16)
    rotated_inputs = jnp.dot(layer_inputs, basis_input, preferred_element_type=jnp.float32).astype(jnp.bfloat16)
    rotated_left = jnp.dot(basis_output.T, query_left, preferred_element_type=jnp.float32).astype(jnp.bfloat16)
    rotated_right = jnp.dot(basis_input.T, query_right, preferred_element_type=jnp.float32).astype(jnp.bfloat16)
    damping = DAMP_RATIO * jnp.sum(eigenvalues.astype(jnp.float32)) / (DG * DA)
    inputs_wide = rotated_inputs.astype(jnp.float32)
    block_size = DG // N_ROW

    def one_query(query_index):
        left_rank = lax.dynamic_slice_in_dim(rotated_left, query_index * RANK, RANK, 1)
        right_rank = lax.dynamic_slice_in_dim(rotated_right, query_index * RANK, RANK, 1)

        def one_block(block_index):
            anchor = block_index * block_size
            left_block = lax.dynamic_slice_in_dim(left_rank, anchor, block_size, 0)
            eigen_block = lax.dynamic_slice_in_dim(eigenvalues, anchor, block_size, 0).astype(jnp.float32)
            grad_block = lax.dynamic_slice_in_dim(rotated_grads, anchor, block_size, 1)
            product = jnp.dot(left_block, right_rank.T, preferred_element_type=jnp.float32)
            precond = (product / (eigen_block + damping)).astype(jnp.bfloat16)
            weighted = jnp.dot(grad_block, precond, preferred_element_type=jnp.float32)
            return jnp.sum(weighted * inputs_wide, axis=1)

        return jnp.sum(lax.map(one_block, jnp.arange(N_ROW, dtype=jnp.int32)), axis=0)

    return lax.map(one_query, jnp.arange(NQ, dtype=jnp.int32))
```

```python
import jax
import jax.numpy as jnp
from jax import lax
from jax.experimental import pallas as pl
from jax.experimental.pallas import tpu as pltpu
from jax.sharding import PartitionSpec as P

DG = 28672
DA = 8192
RANK = 32
NQ = 4
TOK = 512
DAMP_RATIO = 0.1

NX = 4
NZ = 8
KB = 3584
KH = KB // 2
IB = 896
LB = 512
JB = 512
PW = 768
QW = KH - PW
TILE = 256

BF = jnp.bfloat16
F32 = jnp.float32
MESH = pl.DeviceIdType.MESH


def plane_scratch(tag, rows, kind):
    eighth, quarter = rows // 8, rows // 4
    V = pltpu.VMEM
    return {
        tag + "csp": V((2, rows, PW), kind),
        tag + "csq": V((2, rows, QW), kind),
        tag + "crp": V((2, rows, PW), kind),
        tag + "crq": V((2, rows, QW), kind),
        tag + "owp": V((2, rows, PW), F32),
        tag + "owq": V((2, rows, QW), F32),
        tag + "ps": V((2, rows, PW), kind),
        tag + "qs": V((2, 2, NX, eighth, QW), kind),
        tag + "pr": V((2, 3, quarter, PW), kind),
        tag + "qr": V((3, NX, eighth, QW), kind),
        tag + "p2": V((2, 2, eighth, PW), kind),
        tag + "p2f": V((2, 2, eighth, PW), F32),
        tag + "q2": V((NX, eighth, QW), kind),
        tag + "q2f": V((NX, eighth, QW), F32),
        tag + "pr2": V((3, eighth, PW), kind),
        tag + "qr2": V((3, eighth, QW), kind),
        tag + "f": V((2 * rows, KH), kind),
    }


def scratch():
    V = pltpu.VMEM
    shapes = {
        "x": V((TOK, IB), BF),
        "b": V((IB, KB), BF),
        "bin": V((JB, LB), BF),
        "eig": V((KH, LB), BF),
        "ql": V((IB, 128), BF),
        "qr": V((JB, 128), BF),
        "qlt": V((128, IB), BF),
        "y": V((8, 2, 32, JB), BF),
        "qrt": V((128, JB), BF),
        "ads": V((8, 96, 256), BF),
        "adr": V((8, 96, 256), BF),
        "ao": V((8, 80, 256), F32),
        "azs": V((8, 96, 256), BF),
        "azr": V((7, 96, 256), BF),
        "afin": V((2, 8, 80, 256), BF),
        "rm": V((NQ, 128, LB), BF),
        "lt": V((KH, 128), BF),
        "pq": V((NQ, KH, LB), BF),
        "m": V((TOK, 128), F32),
        "dmp": V((4, 8, 128), F32),
        "dmz": V((7, 8, 128), F32),
        "dmx": V((3, 8, 128), F32),
        "dmy": V((3, 8, 128), F32),
        "dmc": V((8, 128), F32),
        "fcs": V((2, 8, 128), F32),
        "fcr": V((8, 128), F32),
        "fzs": V((8, 128), F32),
        "fzr": V((7, 8, 128), F32),
        "fps": V((8, 128), F32),
        "fpr": V((15, 8, 128), F32),
        "fin": V((2, 8, 128), F32),
    }
    shapes.update(plane_scratch("l_", 64, F32))
    shapes.update(plane_scratch("g_", 256, BF))
    return shapes


N_SEM = 144
NAMES = tuple(scratch())


def kernel(xg, yg, b_hbm, bin_hbm, eig_hbm, ql_hbm, qr_hbm, out_ref, *refs):
    s = dict(zip(NAMES, refs))
    send_sems, recv_sems, local_sems = refs[len(NAMES) :]
    d = lax.axis_index("dp")
    r = lax.axis_index("row")
    c = lax.axis_index("col")
    x = c // 4
    yl = lax.rem(c // 2, 2)
    e = lax.rem(c, 2)

    def dev(dp=None, z=None, xx=None, yy=None, ee=None):
        dp = d if dp is None else dp
        z = r if z is None else z
        xx = x if xx is None else xx
        yy = yl if yy is None else yy
        ee = e if ee is None else ee
        return {"dp": dp, "row": z, "col": xx * 4 + yy * 2 + ee}

    def zp(off):
        return lax.rem(r + off, NZ)

    def xp(off):
        return lax.rem(x + off, NX)

    y_peers = ((1 - d, yl), (1 - d, 1 - yl), (d, 1 - yl))

    started = []
    local_started = []

    def send(src, dst, device):
        k = len(started)
        copy = pltpu.make_async_remote_copy(
            src_ref=src,
            dst_ref=dst,
            send_sem=send_sems.at[k],
            recv_sem=recv_sems.at[k],
            device_id=device,
            device_id_type=MESH,
        )
        copy.start()
        started.append(copy)
        return copy

    def fetch(src, dst):
        copy = pltpu.make_async_copy(src, dst, local_sems.at[len(local_started)])
        copy.start()
        local_started.append(copy)
        return copy

    def got(copies):
        for copy in copies:
            copy.wait_recv()

    def aligned(value, step):
        return pl.multiple_of(value, step)

    get_b = fetch(b_hbm, s["b"])
    get_ql = fetch(ql_hbm, s["ql"])
    get_qr = fetch(qr_hbm, s["qr"])
    get_bin = fetch(bin_hbm, s["bin"])
    get_eig = fetch(eig_hbm.at[pl.ds(aligned(d * KH, 256), KH)], s["eig"])

    def slot(z):
        return pl.ds(aligned(lax.rem(z + 4 * e, NZ) * 64, 64), 64)

    get_x = fetch(xg, s["x"].at[slot(r)])
    get_y = fetch(yg, s["y"].at[x * 2 + yl, e])

    barrier = pltpu.get_barrier_semaphore()
    peers = [dev(z=zp(off)) for off in range(1, NZ)]
    for off in range(NX):
        for dp, yy in ((d, yl),) + y_peers:
            if off or dp is not d or yy is not yl:
                peers.append(dev(dp=dp, xx=xp(off), yy=yy))
    peers.append(dev(ee=1 - e))
    for peer in peers:
        pl.semaphore_signal(barrier, inc=1, device_id=peer, device_id_type=MESH)
    pl.semaphore_wait(barrier, len(peers))

    right, left = dev(z=zp(1)), dev(z=zp(NZ - 1))

    def ring(block_right, block_left, part_right=None, part_left=None):
        def rows(z, part):
            base = lax.rem(z + 4 * e, NZ) * 64
            if part is None:
                return pl.ds(aligned(base, 64), 64)
            return pl.ds(aligned(base + part * 32, 32), 32)

        a = rows(block_right, part_right)
        b = rows(block_left, part_left)
        return [
            send(s["x"].at[a], s["x"].at[a], right),
            send(s["x"].at[b], s["x"].at[b], left),
        ]

    get_x.wait()
    z1 = ring(r, r)
    get_y.wait()
    mine = s["y"].at[x * 2 + yl, e]
    y_in = []
    for off in range(NX):
        for yy in (yl, 1 - yl):
            if off or yy is not yl:
                y_in.append(send(mine, mine, dev(xx=xp(off), yy=yy)))

    partner = dev(ee=1 - e)

    def partial_group(tag, rows, lhs, h, q_group):
        width = QW if q_group else PW
        own, out = (s[tag + "owq"], s[tag + "csq"]) if q_group else (s[tag + "owp"], s[tag + "csp"])
        landing = s[tag + "crq"] if q_group else s[tag + "crp"]
        base = h * KH + (PW if q_group else 0)

        def tile(j, carry):
            columns = pl.ds(aligned(base + j * TILE, 128), TILE)
            part = jnp.dot(lhs[...], s["b"][:, columns], preferred_element_type=F32)
            here = pl.ds(aligned(j * TILE, TILE), TILE)
            own[h, :, here] = part[:rows]
            out[h, :, here] = part[rows:].astype(out.dtype)
            return carry

        lax.fori_loop(0, width // TILE, tile, 0)
        return send(out.at[h], landing.at[h], partner)

    def chip_sum(tag, rows, h, q_group):
        eighth = rows // 8
        own = s[tag + "owq"] if q_group else s[tag + "owp"]
        landing = s[tag + "crq"] if q_group else s[tag + "crp"]
        out = s[tag + "qs"] if q_group else s[tag + "ps"]

        def chunk(i, carry):
            here = pl.ds(aligned(i * eighth, eighth), eighth)
            total = own[h, here, :] + landing[h, here, :].astype(F32)
            own[h, here, :] = total
            if q_group:
                out[h, lax.rem(i, 2), i // 2] = total.astype(out.dtype)
            else:
                out[h, here, :] = total.astype(out.dtype)
            return carry

        lax.fori_loop(0, 8, chunk, 0)

    def first_p(tag, rows, h, slot_h):
        quarter = rows // 4
        return [
            send(
                s[tag + "ps"].at[h, pl.ds(aligned(xp(off) * quarter, quarter), quarter)],
                s[tag + "pr"].at[h, off - 1],
                dev(xx=xp(off)),
            )
            for off in range(1, NX)
        ]

    def first_q(tag, which):
        return [
            send(s[tag + "qs"].at[dp, yy], s[tag + "qr"].at[i], dev(dp=dp, yy=yy))
            for i, (dp, yy) in enumerate(y_peers)
            if i in which
        ]

    def second_p(tag, rows, h, which):
        eighth, quarter = rows // 8, rows // 4
        for yy in range(2):
            here = pl.ds(aligned(x * quarter + yy * eighth, eighth), eighth)
            total = s[tag + "owp"][h, here, :]
            for i in range(3):
                total += s[tag + "pr"][h, i, yy * eighth : (yy + 1) * eighth, :].astype(F32)
            s[tag + "p2f"][h, yy] = total
            s[tag + "p2"][h, yy] = total.astype(s[tag + "p2"].dtype)
        return [
            send(s[tag + "p2"].at[dp, yy], s[tag + "pr2"].at[i], dev(dp=dp, yy=yy))
            for i, (dp, yy) in enumerate(y_peers)
            if i in which
        ]

    def second_q(tag, rows):
        eighth, quarter = rows // 8, rows // 4
        for xx in range(NX):
            here = pl.ds(aligned(xx * quarter + yl * eighth, eighth), eighth)
            total = s[tag + "owq"][d, here, :]
            for i in range(3):
                total += s[tag + "qr"][i, xx].astype(F32)
            s[tag + "q2f"][xx] = total
            s[tag + "q2"][xx] = total.astype(s[tag + "q2"].dtype)
        return [
            send(s[tag + "q2"].at[xp(off)], s[tag + "qr2"].at[off - 1], dev(xx=xp(off)))
            for off in range(1, NX)
        ]

    def last_sum(tag, rows):
        eighth, quarter = rows // 8, rows // 4
        here = pl.ds(aligned(e * rows + x * quarter + yl * eighth, eighth), eighth)
        kind = s[tag + "f"].dtype
        p_total = s[tag + "p2f"][d, yl]
        q_total = s[tag + "q2f"][x]
        for i in range(3):
            p_total += s[tag + "pr2"][i].astype(F32)
            q_total += s[tag + "qr2"][i].astype(F32)
        s[tag + "f"][here, :PW] = p_total.astype(kind)
        s[tag + "f"][here, PW:] = q_total.astype(kind)
        block = s[tag + "f"].at[here]
        copies = []
        for off in range(NX):
            for yy in (yl, 1 - yl):
                if off or yy is not yl:
                    copies.append(send(block, block, dev(xx=xp(off), yy=yy)))
        return copies

    def to_partner(tag, rows):
        block = s[tag + "f"].at[pl.ds(aligned(e * rows, rows), rows)]
        return [send(block, block, partner)]

    groups = ((1 - d, True), (1 - d, False), (d, True), (d, False))

    get_ql.wait()
    turned = s["ql"][...].astype(F32).T.astype(BF)
    s["qlt"][:64] = jnp.where(e == 0, turned[:64], turned[64:])
    s["qlt"][64:] = jnp.where(e == 0, turned[64:], turned[:64])
    get_qr.wait()
    s["qrt"][...] = s["qr"][...].astype(F32).T.astype(BF)
    get_b.wait()
    l_core = [partial_group("l_", 64, s["qlt"], h, q) for h, q in groups[:2]]
    got(z1)
    z2 = ring(zp(NZ - 1), zp(1))
    l_core += [partial_group("l_", 64, s["qlt"], h, q) for h, q in groups[2:]]

    get_eig.wait()

    def eig_sum(i, total):
        rows = s["eig"][pl.ds(aligned(i * 128, 128), 128), :].astype(F32)
        return total + jnp.sum(rows.reshape(16, 8, LB), axis=0)

    total = lax.fori_loop(0, KH // 128, eig_sum, jnp.zeros((8, LB), F32))
    s["dmp"][0] = total[:, :128] + total[:, 128:256] + total[:, 256:384] + total[:, 384:]
    dm_z = [send(s["dmp"].at[0], s["dmz"].at[off - 1], dev(z=zp(off))) for off in range(1, NZ)]

    def run_plane_first(tag, rows, core_copies):
        copies_q, copies_p = [], []
        for i, (h, q_group) in enumerate(groups):
            got([core_copies[i]])
            chip_sum(tag, rows, h, q_group)
            if q_group:
                copies_q += first_q(tag, (0, 1) if i == 0 else (2,))
            else:
                copies_p.append(first_p(tag, rows, h, i))
        return copies_q, copies_p

    l_q, l_p = run_plane_first("l_", 64, l_core)
    got(z2)
    z3 = ring(zp(NZ - 2), zp(2))

    got(y_in)
    y_half = s["y"].at[:, e]
    y_core = [send(y_half, y_half, partner)]

    got(dm_z)
    s["dmp"][1] = s["dmp"][0] + jnp.sum(s["dmz"][...], axis=0)
    dm_x = [send(s["dmp"].at[1], s["dmx"].at[off - 1], dev(xx=xp(off))) for off in range(1, NX)]

    got(l_q)
    l_q2 = second_q("l_", 64)
    got(l_p[0])
    l_p2 = second_p("l_", 64, 1 - d, (0, 1))
    got(l_p[1])
    l_p2 += second_p("l_", 64, d, (2,))

    got(z3)
    z4 = ring(zp(NZ - 3), zp(3), 0, 1)

    got(y_core)
    get_bin.wait()
    tokens = s["y"][...].reshape(TOK, JB)

    def input_parts(half):
        columns = pl.ds(aligned(half * 256, 256), 256)
        basis = s["bin"][:, columns]
        return (
            jnp.dot(tokens, basis, preferred_element_type=F32),
            jnp.dot(s["qrt"][...], basis, preferred_element_type=F32),
        )

    def put(dst, g, token_rows, factor_rows):
        dst[g, :64] = token_rows.astype(BF)
        high = factor_rows.astype(BF)
        dst[g, 64:80] = high
        dst[g, 80:] = (factor_rows - high.astype(F32)).astype(BF)

    token_part, factor_part = input_parts(1 - d)
    for g in range(8):
        put(s["ads"], g, token_part[g * 64 : (g + 1) * 64], factor_part[g * 16 : (g + 1) * 16])
    a_dp = [send(s["ads"], s["adr"], dev(dp=1 - d))]
    token_part, factor_part = input_parts(d)
    for g in range(8):
        s["ao"][g, :64] = token_part[g * 64 : (g + 1) * 64]
        s["ao"][g, 64:] = factor_part[g * 16 : (g + 1) * 16]

    got(dm_x)
    s["dmp"][2] = s["dmp"][1] + jnp.sum(s["dmx"][...], axis=0)
    dm_y = [
        send(s["dmp"].at[2], s["dmy"].at[i], dev(dp=dp, yy=yy)) for i, (dp, yy) in enumerate(y_peers)
    ]

    got(l_q2)
    got(l_p2)
    l_f = last_sum("l_", 64)

    got(z4)
    g_core = [partial_group("g_", 256, s["x"], *groups[0])]
    g_q, g_p = [], []
    for i, (h, q_group) in enumerate(groups):
        if i + 1 < len(groups):
            g_core.append(partial_group("g_", 256, s["x"], *groups[i + 1]))
        got([g_core[i]])
        chip_sum("g_", 256, h, q_group)
        if q_group:
            g_q += first_q("g_", (0, 1) if i == 0 else (2,))
        else:
            g_p.append(first_p("g_", 256, h, i))

    got(a_dp)

    def a_first(g, carry):
        landed = s["adr"]
        token_rows = s["ao"][g, :64] + landed[g, :64].astype(F32)
        factor_rows = s["ao"][g, 64:] + landed[g, 64:80].astype(F32) + landed[g, 80:].astype(F32)
        s["ao"][g, :64] = token_rows
        s["ao"][g, 64:] = factor_rows
        put(s["azs"], g, token_rows, factor_rows)
        return carry

    lax.fori_loop(0, 8, a_first, 0)
    a_z = [send(s["azs"].at[zp(off)], s["azr"].at[off - 1], dev(z=zp(off))) for off in range(1, NZ)]

    got(l_f)
    l_last = to_partner("l_", 64)
    got(dm_y)
    s["dmp"][3] = s["dmp"][2] + jnp.sum(s["dmy"][...], axis=0)
    dm_c = [send(s["dmp"].at[3], s["dmc"], partner)]

    got(a_z)
    token_rows = s["ao"][r, :64]
    factor_rows = s["ao"][r, 64:]
    for i in range(7):
        token_rows += s["azr"][i, :64].astype(F32)
        factor_rows += s["azr"][i, 64:80].astype(F32) + s["azr"][i, 80:].astype(F32)
    s["afin"][d, r, :64] = token_rows.astype(BF)
    s["afin"][d, r, 64:] = factor_rows.astype(BF)
    mine = s["afin"].at[d, r]
    a_f = [send(mine, mine, dev(z=zp(off))) for off in range(1, NZ)]

    got(g_q)
    g_q2 = second_q("g_", 256)
    got(g_p[0])
    g_p2 = second_p("g_", 256, 1 - d, (0, 1))
    got(g_p[1])
    g_p2 += second_p("g_", 256, d, (2,))

    got(a_f)
    mine = s["afin"].at[d]
    a_last = [send(mine, mine, dev(dp=1 - d))]

    got(g_q2)
    got(g_p2)
    g_f = last_sum("g_", 256)

    got(dm_c)
    damping = jnp.sum(s["dmp"][3] + s["dmc"][...], keepdims=True) * (DAMP_RATIO / (DG * DA))
    got(l_last)
    s["lt"][...] = s["l_f"][...].T.astype(BF)
    got(a_last)
    for q in range(NQ):
        s["rm"][q] = jnp.zeros((128, LB), BF)
        for g in range(2):
            rows = slice(q * RANK + g * 16, q * RANK + (g + 1) * 16)
            for half in range(2):
                s["rm"][q, rows, half * 256 : (half + 1) * 256] = s["afin"][half, q * 2 + g, 64:]

    def precondition(i, carry):
        rows = pl.ds(aligned(i * 128, 128), 128)
        inverse = 1.0 / (s["eig"][rows, :].astype(F32) + damping)
        left_rows = s["lt"][rows, :]
        for q in range(NQ):
            product = jnp.dot(left_rows, s["rm"][q], preferred_element_type=F32)
            s["pq"][q, rows, :] = (product * inverse).astype(BF)
        return carry

    lax.fori_loop(0, KH // 128, precondition, 0)

    got(g_f)
    g_last = to_partner("g_", 256)
    lanes = lax.broadcasted_iota(jnp.int32, (TILE, 128), 1)
    token_group = lax.broadcasted_iota(jnp.int32, (TILE, 128), 0) // 128

    def score(half):
        here = pl.ds(aligned(half * 256, 256), 256)
        s["m"][here, :] = jnp.zeros((TILE, 128), F32)

        def one_query(q, carry):
            weighted = jnp.dot(s["g_f"][here, :], s["pq"][q], preferred_element_type=F32)
            total = jnp.zeros((TILE, 128), F32)
            for part in range(2):
                inputs = s["afin"][part, pl.ds(half * 4, 4), :64, :].astype(F32).reshape(TILE, 256)
                terms = weighted[:, part * 256 : (part + 1) * 256] * inputs
                total += terms[:, :128] + terms[:, 128:]
            scores = jnp.sum(total, axis=1, keepdims=True)
            s["m"][here, :] += jnp.where(lanes == q + 4 * token_group, scores, 0.0)
            return carry

        lax.fori_loop(0, NQ, one_query, 0)

    score(e)
    got(g_last)
    score(1 - e)

    turned = s["m"][...].T[:8]
    for half in range(2):
        base = half * 256
        s["fcs"][half] = turned[:, base : base + 128] + turned[:, base + 128 : base + 256]
    f_core = [send(s["fcs"].at[1 - e], s["fcr"], partner)]
    got(f_core)
    s["fzs"][...] = s["fcs"][e] + s["fcr"][...]
    f_z = [send(s["fzs"], s["fzr"].at[off - 1], dev(z=zp(off))) for off in range(1, NZ)]
    got(f_z)
    s["fps"][...] = s["fzs"][...] + jnp.sum(s["fzr"][...], axis=0)
    f_plane = []
    for off in range(NX):
        for dp, yy in ((d, yl),) + y_peers:
            if off or dp is not d or yy is not yl:
                f_plane.append(send(s["fps"], s["fpr"].at[len(f_plane)], dev(dp=dp, xx=xp(off), yy=yy)))
    got(f_plane)
    s["fin"][e] = s["fps"][...] + jnp.sum(s["fpr"][...], axis=0)
    mine = s["fin"].at[e]
    f_last = [send(mine, mine, partner)]
    got(f_last)
    for half in range(2):
        for part in range(2):
            columns = slice((half * 2 + part) * 128, (half * 2 + part + 1) * 128)
            low = s["fin"][half, part * 4 : part * 4 + 2, :]
            high = s["fin"][half, part * 4 + 2 : part * 4 + 4, :]
            out_ref[:, columns] = jnp.where(d == 0, low, high)

    for copy in started:
        copy.wait_send()


def local(out_grads, layer_inputs, basis_output, basis_input, eigenvalues, query_left, query_right):
    any_space = pl.BlockSpec(memory_space=pl.ANY)
    return pl.pallas_call(
        kernel,
        out_shape=jax.ShapeDtypeStruct((2, TOK), F32),
        in_specs=[any_space] * 7,
        out_specs=pl.BlockSpec(memory_space=pltpu.VMEM),
        scratch_shapes=list(scratch().values())
        + [
            pltpu.SemaphoreType.DMA((N_SEM,)),
            pltpu.SemaphoreType.DMA((N_SEM,)),
            pltpu.SemaphoreType.DMA((8,)),
        ],
        compiler_params=pltpu.CompilerParams(
            collective_id=0, has_side_effects=True, vmem_limit_bytes=60 * 1024 * 1024
        ),
        cost_estimate=pl.CostEstimate(flops=9_000_000_000, bytes_accessed=11_000_000, transcendentals=0),
    )(out_grads, layer_inputs, basis_output, basis_input, eigenvalues, query_left, query_right)


def solution(mesh):
    in_specs = (
        P("row", ("dp", "col")),
        P("col", ("dp", "row")),
        P(("dp", "col"), "row"),
        P(("dp", "row"), "col"),
        P("row", "col"),
        P(("dp", "col"), None),
        P(("dp", "row"), None),
    )
    return jax.shard_map(
        local, mesh=mesh, in_specs=in_specs, out_specs=P("dp", None), check_vma=False
    )
```

```python
import jax
import jax.numpy as jnp
from jax import lax
from jax.experimental import pallas as pl
from jax.experimental.pallas import tpu as pltpu
from jax.sharding import PartitionSpec as P

DG = 28672
DA = 8192
RANK = 32
NQ = 4
TOK = 512
DAMP_RATIO = 0.1

NX = 4
NZ = 8
KB = 3584
KH = KB // 2
IB = 896
LB = 512
JB = 512
PW = 768
QW = KH - PW
TILE = 256
ROWS = 128
ORDER = (0, -1, 1, -2, 2, -3, 3, 4)

BF = jnp.bfloat16
F32 = jnp.float32
MESH = pl.DeviceIdType.MESH


def plane_scratch(tag, rows, kind):
    eighth, quarter = rows // 8, rows // 4
    V = pltpu.VMEM
    return {
        tag + "csp": V((2, rows, PW), kind),
        tag + "csq": V((2, rows, QW), kind),
        tag + "crp": V((2, rows, PW), kind),
        tag + "crq": V((2, rows, QW), kind),
        tag + "owp": V((2, rows, PW), F32),
        tag + "owq": V((2, rows, QW), F32),
        tag + "ps": V((2, rows, PW), kind),
        tag + "qs": V((2, 2, NX, eighth, QW), kind),
        tag + "pr": V((2, 3, quarter, PW), kind),
        tag + "qr": V((3, NX, eighth, QW), kind),
        tag + "p2": V((2, 2, eighth, PW), kind),
        tag + "p2f": V((2, 2, eighth, PW), F32),
        tag + "q2": V((NX, eighth, QW), kind),
        tag + "q2f": V((NX, eighth, QW), F32),
        tag + "pr2": V((3, eighth, PW), kind),
        tag + "qr2": V((3, eighth, QW), kind),
        tag + "f": V((2 * rows, KH), BF) if rows >= 128 else V((16, 16, KH // 2), BF),
    }


def scratch():
    V = pltpu.VMEM
    shapes = {
        "x": V((2, 2 * ROWS, IB), BF),
        "b": V((IB, KB), BF),
        "bin": V((JB, LB), BF),
        "eig": V((KH, LB), BF),
        "ql": V((IB, 128), BF),
        "qr": V((JB, 128), BF),
        "qlt": V((128, IB), BF),
        "y": V((8, 2, 32, JB), BF),
        "qrt": V((128, JB), BF),
        "rs": V((8, 16, 256), F32),
        "rr": V((8, 16, 256), F32),
        "ro": V((8, 16, 256), F32),
        "rzr": V((7, 16, 256), F32),
        "rfin": V((2, 8, 16, 256), BF),
        "ads": V((8, 64, 256), BF),
        "adr": V((8, 64, 256), BF),
        "ao": V((8, 64, 256), F32),
        "azs": V((8, 64, 256), BF),
        "azr": V((7, 64, 256), BF),
        "afin": V((2, 8, 64, 256), BF),
        "rm": V((NQ, 128, LB), BF),
        "lt": V((KH, 128), BF),
        "pq": V((NQ, KH, LB), BF),
        "at": V((2 * ROWS, LB), F32),
        "mc": V((2 * ROWS, 128), F32),
        "m": V((TOK, 128), F32),
        "dmp": V((4, 8, 128), F32),
        "dmz": V((7, 8, 128), F32),
        "dmx": V((3, 8, 128), F32),
        "dmy": V((3, 8, 128), F32),
        "dmc": V((8, 128), F32),
        "fcs": V((2, 8, 128), F32),
        "fcr": V((8, 128), F32),
        "fzs": V((8, 128), F32),
        "fzr": V((7, 8, 128), F32),
        "fps": V((8, 128), F32),
        "fpr": V((15, 8, 128), F32),
        "fin": V((2, 8, 128), F32),
    }
    shapes.update(plane_scratch("l_", 64, F32))
    shapes.update(plane_scratch("a_", ROWS, BF))
    shapes.update(plane_scratch("b_", ROWS, BF))
    return shapes


N_SEM = 176
NAMES = tuple(scratch())


def kernel(xg, yg, b_hbm, bin_hbm, eig_hbm, ql_hbm, qr_hbm, out_ref, *refs):
    s = dict(zip(NAMES, refs))
    send_sems, recv_sems, local_sems = refs[len(NAMES) :]
    d = lax.axis_index("dp")
    r = lax.axis_index("row")
    c = lax.axis_index("col")
    x = c // 4
    yl = lax.rem(c // 2, 2)
    e = lax.rem(c, 2)

    def dev(dp=None, z=None, xx=None, yy=None, ee=None):
        dp = d if dp is None else dp
        z = r if z is None else z
        xx = x if xx is None else xx
        yy = yl if yy is None else yy
        ee = e if ee is None else ee
        return {"dp": dp, "row": z, "col": xx * 4 + yy * 2 + ee}

    def zp(off):
        return lax.rem(r + off, NZ)

    def xp(off):
        return lax.rem(x + off, NX)

    y_peers = ((1 - d, yl), (1 - d, 1 - yl), (d, 1 - yl))

    started = []
    local_started = []

    def send(src, dst, device):
        k = len(started)
        copy = pltpu.make_async_remote_copy(
            src_ref=src,
            dst_ref=dst,
            send_sem=send_sems.at[k],
            recv_sem=recv_sems.at[k],
            device_id=device,
            device_id_type=MESH,
        )
        copy.start()
        started.append(copy)
        return copy

    def fetch(src, dst):
        copy = pltpu.make_async_copy(src, dst, local_sems.at[len(local_started)])
        copy.start()
        local_started.append(copy)
        return copy

    def got(copies):
        for copy in copies:
            copy.wait_recv()

    def aligned(value, step):
        return pl.multiple_of(value, step)

    get_b = fetch(b_hbm, s["b"])
    get_ql = fetch(ql_hbm, s["ql"])
    get_qr = fetch(qr_hbm, s["qr"])
    get_bin = fetch(bin_hbm, s["bin"])
    get_eig = fetch(eig_hbm.at[pl.ds(aligned(d * KH, 256), KH)], s["eig"])

    def place(rel, part=None):
        position = ORDER.index(rel)
        base = lax.rem(position % 4 + 2 * e, 4) * 64
        if part is None:
            return s["x"].at[position // 4, pl.ds(aligned(base, 64), 64)]
        return s["x"].at[position // 4, pl.ds(aligned(base + part * 32, 32), 32)]

    get_x = fetch(xg, place(0))
    get_y = fetch(yg, s["y"].at[x * 2 + yl, e])

    barrier = pltpu.get_barrier_semaphore()
    peers = [dev(z=zp(off)) for off in range(1, NZ)]
    for off in range(NX):
        for dp, yy in ((d, yl),) + y_peers:
            if off or dp is not d or yy is not yl:
                peers.append(dev(dp=dp, xx=xp(off), yy=yy))
    peers.append(dev(ee=1 - e))
    for peer in peers:
        pl.semaphore_signal(barrier, inc=1, device_id=peer, device_id_type=MESH)
    right, left = dev(z=zp(1)), dev(z=zp(NZ - 1))

    def along_z(distance, parts_right=(0, 1), parts_left=(0, 1)):
        copies = []
        for part in range(2):
            if distance:
                got(z_in[part])
            if part in parts_right:
                far = 4 if distance == 3 else -distance - 1
                copies.append([send(place(-distance, part), place(far, part), right)])
            else:
                copies.append([])
            if part in parts_left:
                copies[-1].append(send(place(distance, part), place(distance + 1, part), left))
        return copies

    partner = dev(ee=1 - e)

    def partial_group(tag, rows, lhs, h, q_group):
        width = QW if q_group else PW
        own, out = (s[tag + "owq"], s[tag + "csq"]) if q_group else (s[tag + "owp"], s[tag + "csp"])
        landing = s[tag + "crq"] if q_group else s[tag + "crp"]
        base = h * KH + (PW if q_group else 0)

        def tile(j, carry):
            columns = pl.ds(aligned(base + j * TILE, 128), TILE)
            part = jnp.dot(lhs[...], s["b"][:, columns], preferred_element_type=F32)
            here = pl.ds(aligned(j * TILE, TILE), TILE)
            own[h, :, here] = part[:rows]
            out[h, :, here] = part[rows:].astype(out.dtype)
            return carry

        lax.fori_loop(0, width // TILE, tile, 0)
        return lambda: send(out.at[h], landing.at[h], partner)

    def chip_sum(tag, rows, h, q_group):
        eighth = rows // 8
        own = s[tag + "owq"] if q_group else s[tag + "owp"]
        landing = s[tag + "crq"] if q_group else s[tag + "crp"]
        out = s[tag + "qs"] if q_group else s[tag + "ps"]

        def chunk(i, carry):
            here = pl.ds(aligned(i * eighth, eighth), eighth)
            total = own[h, here, :] + landing[h, here, :].astype(F32)
            own[h, here, :] = total
            if q_group:
                out[h, lax.rem(i, 2), i // 2] = total.astype(out.dtype)
            else:
                out[h, here, :] = total.astype(out.dtype)
            return carry

        lax.fori_loop(0, 8, chunk, 0)

    def first_p(tag, rows, h, slot_h):
        quarter = rows // 4
        return [
            send(
                s[tag + "ps"].at[h, pl.ds(aligned(xp(off) * quarter, quarter), quarter)],
                s[tag + "pr"].at[h, off - 1],
                dev(xx=xp(off)),
            )
            for off in range(1, NX)
        ]

    def first_q(tag, which):
        return [
            send(s[tag + "qs"].at[dp, yy], s[tag + "qr"].at[i], dev(dp=dp, yy=yy))
            for i, (dp, yy) in enumerate(y_peers)
            if i in which
        ]

    def second_p(tag, rows, h, which):
        eighth, quarter = rows // 8, rows // 4
        for yy in range(2):
            here = pl.ds(aligned(x * quarter + yy * eighth, eighth), eighth)
            total = s[tag + "owp"][h, here, :]
            for i in range(3):
                total += s[tag + "pr"][h, i, yy * eighth : (yy + 1) * eighth, :].astype(F32)
            s[tag + "p2f"][h, yy] = total
            s[tag + "p2"][h, yy] = total.astype(s[tag + "p2"].dtype)
        return [
            send(s[tag + "p2"].at[dp, yy], s[tag + "pr2"].at[i], dev(dp=dp, yy=yy))
            for i, (dp, yy) in enumerate(y_peers)
            if i in which
        ]

    def second_q(tag, rows):
        eighth, quarter = rows // 8, rows // 4
        for xx in range(NX):
            here = pl.ds(aligned(xx * quarter + yl * eighth, eighth), eighth)
            total = s[tag + "owq"][d, here, :]
            for i in range(3):
                total += s[tag + "qr"][i, xx].astype(F32)
            s[tag + "q2f"][xx] = total
            s[tag + "q2"][xx] = total.astype(s[tag + "q2"].dtype)
        return [
            send(s[tag + "q2"].at[xp(off)], s[tag + "qr2"].at[off - 1], dev(xx=xp(off)))
            for off in range(1, NX)
        ]

    def last_sum(tag, rows):
        eighth, quarter = rows // 8, rows // 4
        here = pl.ds(aligned(e * rows + x * quarter + yl * eighth, eighth), eighth)
        p_total = s[tag + "p2f"][d, yl]
        q_total = s[tag + "q2f"][x]
        for i in range(3):
            p_total += s[tag + "pr2"][i].astype(F32)
            q_total += s[tag + "qr2"][i].astype(F32)
        if rows >= 128:
            s[tag + "f"][here, :PW] = p_total.astype(BF)
            s[tag + "f"][here, PW:] = q_total.astype(BF)
            block = s[tag + "f"].at[here]
        else:
            whole = jnp.concatenate([p_total, q_total], axis=1)
            halves = [whole[:, : KH // 2], whole[:, KH // 2 :]]
            s[tag + "f"][e * 8 + x * 2 + yl] = jnp.concatenate(halves, axis=0).astype(BF)
            block = s[tag + "f"].at[e * 8 + x * 2 + yl]
        copies = []
        for off in range(NX):
            for yy in (yl, 1 - yl):
                if off or yy is not yl:
                    copies.append(send(block, block, dev(xx=xp(off), yy=yy)))
        return copies

    def to_partner(tag, rows):
        count = rows if rows >= 128 else 8
        block = s[tag + "f"].at[pl.ds(aligned(e * count, count), count)]
        return [send(block, block, partner)]

    groups = ((1 - d, True), (1 - d, False), (d, True), (d, False))

    get_ql.wait()
    turned = s["ql"][...].astype(F32).T.astype(BF)
    s["qlt"][:64] = jnp.where(e == 0, turned[:64], turned[64:])
    s["qlt"][64:] = jnp.where(e == 0, turned[64:], turned[:64])
    get_qr.wait()
    s["qrt"][...] = s["qr"][...].astype(F32).T.astype(BF)
    get_x.wait()
    get_y.wait()
    get_b.wait()
    l_ready = [partial_group("l_", 64, s["qlt"], h, q) for h, q in groups[:2]]
    pl.semaphore_wait(barrier, len(peers))

    z_in = along_z(0)
    mine = s["y"].at[x * 2 + yl, e]
    y_in = []
    for off in range(NX):
        for yy in (yl, 1 - yl):
            if off or yy is not yl:
                y_in.append(send(mine, mine, dev(xx=xp(off), yy=yy)))
    l_core = [start() for start in l_ready]

    def half_columns(half):
        return pl.ds(aligned(half * 256, 256), 256)

    get_bin.wait()
    factor_part = jnp.dot(s["qrt"][...], s["bin"][:, half_columns(1 - d)], preferred_element_type=F32)
    s["rs"][...] = factor_part.reshape(8, 16, 256)
    r_dp = [send(s["rs"], s["rr"], dev(dp=1 - d))]
    factor_part = jnp.dot(s["qrt"][...], s["bin"][:, half_columns(d)], preferred_element_type=F32)
    s["ro"][...] = factor_part.reshape(8, 16, 256)

    l_core += [partial_group("l_", 64, s["qlt"], h, q)() for h, q in groups[2:]]

    def first_steps(tag, rows, core_copies, i):
        h, q_group = groups[i]
        got([core_copies[i]])
        chip_sum(tag, rows, h, q_group)
        if q_group:
            return first_q(tag, (0, 1) if i == 0 else (2,))
        return first_p(tag, rows, h, i)

    l_first = [first_steps("l_", 64, l_core, i) for i in range(4)]
    z_in = along_z(1)
    got(y_in)
    y_half = s["y"].at[:, e]
    y_core = [send(y_half, y_half, partner)]

    get_eig.wait()

    def eig_sum(i, total):
        rows = s["eig"][pl.ds(aligned(i * 128, 128), 128), :].astype(F32)
        return total + jnp.sum(rows.reshape(16, 8, LB), axis=0)

    total = lax.fori_loop(0, KH // 128, eig_sum, jnp.zeros((8, LB), F32))
    s["dmp"][0] = total[:, :128] + total[:, 128:256] + total[:, 256:384] + total[:, 384:]
    dm_z = [send(s["dmp"].at[0], s["dmz"].at[off - 1], dev(z=zp(off))) for off in range(1, NZ)]

    got(r_dp)
    s["ro"][...] += s["rr"][...]
    r_z = [send(s["ro"].at[zp(off)], s["rzr"].at[off - 1], dev(z=zp(off))) for off in range(1, NZ)]

    got(y_core)
    token_part = jnp.dot(
        s["y"][...].reshape(TOK, JB), s["bin"][:, half_columns(1 - d)], preferred_element_type=F32
    )
    s["ads"][...] = token_part.reshape(8, 64, 256).astype(BF)
    a_dp = [send(s["ads"], s["adr"], dev(dp=1 - d))]
    token_part = jnp.dot(
        s["y"][...].reshape(TOK, JB), s["bin"][:, half_columns(d)], preferred_element_type=F32
    )
    s["ao"][...] = token_part.reshape(8, 64, 256)

    z_in = along_z(2)

    a_core, a_first_in = [], []
    for i in range(2):
        a_core.append(partial_group("a_", ROWS, s["x"].at[0], *groups[i])())
    a_first_in.append(first_steps("a_", ROWS, a_core, 0))
    z_in = along_z(3, (0,), (1,))
    for i in range(2, 4):
        a_core.append(partial_group("a_", ROWS, s["x"].at[0], *groups[i])())
        a_first_in.append(first_steps("a_", ROWS, a_core, i - 1))
    a_first_in.append(first_steps("a_", ROWS, a_core, 3))

    got(a_dp)
    summed = s["ao"][...] + s["adr"][...].astype(F32)
    s["ao"][...] = summed
    s["azs"][...] = summed.astype(BF)
    a_z = [send(s["azs"].at[zp(off)], s["azr"].at[off - 1], dev(z=zp(off))) for off in range(1, NZ)]

    got(dm_z)
    s["dmp"][1] = s["dmp"][0] + jnp.sum(s["dmz"][...], axis=0)
    dm_x = [send(s["dmp"].at[1], s["dmx"].at[off - 1], dev(xx=xp(off))) for off in range(1, NX)]

    def second_steps(tag, rows, first):
        got(first[0])
        got(first[2])
        copies = second_q(tag, rows)
        got(first[1])
        copies += second_p(tag, rows, 1 - d, (0, 1))
        got(first[3])
        return copies + second_p(tag, rows, d, (2,))

    l_second = second_steps("l_", 64, l_first)

    got(z_in[0])
    got(z_in[1])
    b_core, b_first_in = [], []
    for i in range(4):
        b_core.append(partial_group("b_", ROWS, s["x"].at[1], *groups[i])())
        if i:
            b_first_in.append(first_steps("b_", ROWS, b_core, i - 1))
    b_first_in.append(first_steps("b_", ROWS, b_core, 3))

    got(r_z)
    factors = s["ro"][r] + jnp.sum(s["rzr"][...], axis=0)
    s["rfin"][d, r] = factors.astype(BF)
    mine = s["rfin"].at[d, r]
    r_f = [send(mine, mine, dev(z=zp(off))) for off in range(1, NZ)]

    got(dm_x)
    s["dmp"][2] = s["dmp"][1] + jnp.sum(s["dmx"][...], axis=0)
    dm_y = [
        send(s["dmp"].at[2], s["dmy"].at[i], dev(dp=dp, yy=yy)) for i, (dp, yy) in enumerate(y_peers)
    ]

    got(l_second)
    l_f = last_sum("l_", 64)

    a_second = second_steps("a_", ROWS, a_first_in)

    got(a_z)
    summed = s["ao"][r]
    for i in range(7):
        summed += s["azr"][i].astype(F32)
    s["afin"][d, r] = summed.astype(BF)
    mine = s["afin"].at[d, r]
    a_f = [send(mine, mine, dev(z=zp(off))) for off in range(1, NZ)]

    got(r_f)
    mine = s["rfin"].at[d]
    r_last = [send(mine, mine, dev(dp=1 - d))]
    got(dm_y)
    s["dmp"][3] = s["dmp"][2] + jnp.sum(s["dmy"][...], axis=0)
    dm_c = [send(s["dmp"].at[3], s["dmc"], partner)]
    got(l_f)
    l_last = to_partner("l_", 64)

    got(a_second)
    a_out = last_sum("a_", ROWS)

    b_second = second_steps("b_", ROWS, b_first_in)

    got(dm_c)
    damping = jnp.sum(s["dmp"][3] + s["dmc"][...], keepdims=True) * (DAMP_RATIO / (DG * DA))
    got(l_last)
    for i in range(2):
        left_rows = s["l_f"][...].astype(F32)[:, i * 8 : (i + 1) * 8].reshape(128, KH // 2)
        s["lt"][i * (KH // 2) : (i + 1) * (KH // 2)] = left_rows.T.astype(BF)
    got(r_last)
    for q in range(NQ):
        s["rm"][q] = jnp.zeros((128, LB), BF)
        for g in range(2):
            rows = slice(q * RANK + g * 16, q * RANK + (g + 1) * 16)
            for half in range(2):
                s["rm"][q, rows, half * 256 : (half + 1) * 256] = s["rfin"][half, q * 2 + g]

    def precondition(i, carry):
        rows = pl.ds(aligned(i * 128, 128), 128)
        inverse = 1.0 / (s["eig"][rows, :].astype(F32) + damping)
        left_rows = s["lt"][rows, :]
        for q in range(NQ):
            product = jnp.dot(left_rows, s["rm"][q], preferred_element_type=F32)
            s["pq"][q, rows, :] = (product * inverse).astype(BF)
        return carry

    lax.fori_loop(0, KH // 128, precondition, 0)

    got(a_f)
    mine = s["afin"].at[d]
    a_last = [send(mine, mine, dev(dp=1 - d))]

    got(b_second)
    b_out = last_sum("b_", ROWS)

    got(a_out)
    a_both = to_partner("a_", ROWS)
    got(a_last)

    lanes = lax.broadcasted_iota(jnp.int32, (2 * ROWS, 128), 1)
    block_of = lax.broadcasted_iota(jnp.int32, (2 * ROWS, 128), 0) // 64

    def score(tag, chunk):
        blocks = [lax.rem(r + ORDER[chunk * 4 + j] + NZ, NZ) for j in range(4)]
        odd = jnp.zeros_like(lanes)
        for j, block in enumerate(blocks):
            odd = jnp.where(block_of == j, lax.rem(block // 2, 2), odd)
            for half in range(2):
                columns = slice(half * 256, (half + 1) * 256)
                s["at"][j * 64 : (j + 1) * 64, columns] = s["afin"][half, block].astype(F32)
        s["mc"][...] = jnp.zeros((2 * ROWS, 128), F32)

        def one_query(q, carry):
            weighted = jnp.dot(s[tag + "f"][...], s["pq"][q], preferred_element_type=F32)
            terms = weighted * s["at"][...]
            total = terms[:, :128] + terms[:, 128:256] + terms[:, 256:384] + terms[:, 384:]
            scores = jnp.sum(total, axis=1, keepdims=True)
            s["mc"][...] += jnp.where(lanes == q + 4 * odd, scores, 0.0)
            return carry

        lax.fori_loop(0, NQ, one_query, 0)
        for j, block in enumerate(blocks):
            s["m"][pl.ds(aligned(block * 64, 64), 64), :] = s["mc"][j * 64 : (j + 1) * 64, :]

    got(a_both)
    score("a_", 0)
    drained = len(started)
    for copy in started[: drained - 8]:
        copy.wait_send()
    got(b_out)
    b_both = to_partner("b_", ROWS)
    got(b_both)
    score("b_", 1)

    turned = s["m"][...].T[:8]
    for half in range(2):
        base = half * 256
        s["fcs"][half] = turned[:, base : base + 128] + turned[:, base + 128 : base + 256]
    f_core = [send(s["fcs"].at[1 - e], s["fcr"], partner)]
    got(f_core)
    s["fzs"][...] = s["fcs"][e] + s["fcr"][...]
    f_z = [send(s["fzs"], s["fzr"].at[off - 1], dev(z=zp(off))) for off in range(1, NZ)]
    got(f_z)
    s["fps"][...] = s["fzs"][...] + jnp.sum(s["fzr"][...], axis=0)
    f_plane = []
    for off in range(NX):
        for dp, yy in ((d, yl),) + y_peers:
            if off or dp is not d or yy is not yl:
                f_plane.append(send(s["fps"], s["fpr"].at[len(f_plane)], dev(dp=dp, xx=xp(off), yy=yy)))
    got(f_plane)
    s["fin"][e] = s["fps"][...] + jnp.sum(s["fpr"][...], axis=0)
    mine = s["fin"].at[e]
    f_last = [send(mine, mine, partner)]
    got(f_last)
    for half in range(2):
        for part in range(2):
            columns = slice((half * 2 + part) * 128, (half * 2 + part + 1) * 128)
            low = s["fin"][half, part * 4 : part * 4 + 2, :]
            high = s["fin"][half, part * 4 + 2 : part * 4 + 4, :]
            out_ref[:, columns] = jnp.where(d == 0, low, high)

    for copy in started[drained - 8 :]:
        copy.wait_send()


def local(out_grads, layer_inputs, basis_output, basis_input, eigenvalues, query_left, query_right):
    any_space = pl.BlockSpec(memory_space=pl.ANY)
    return pl.pallas_call(
        kernel,
        out_shape=jax.ShapeDtypeStruct((2, TOK), F32),
        in_specs=[any_space] * 7,
        out_specs=pl.BlockSpec(memory_space=pltpu.VMEM),
        scratch_shapes=list(scratch().values())
        + [
            pltpu.SemaphoreType.DMA((N_SEM,)),
            pltpu.SemaphoreType.DMA((N_SEM,)),
            pltpu.SemaphoreType.DMA((8,)),
        ],
        compiler_params=pltpu.CompilerParams(
            collective_id=0, has_side_effects=True, vmem_limit_bytes=60 * 1024 * 1024
        ),
        cost_estimate=pl.CostEstimate(flops=9_000_000_000, bytes_accessed=11_000_000, transcendentals=0),
    )(out_grads, layer_inputs, basis_output, basis_input, eigenvalues, query_left, query_right)


def solution(mesh):
    in_specs = (
        P("row", ("dp", "col")),
        P("col", ("dp", "row")),
        P(("dp", "col"), "row"),
        P(("dp", "row"), "col"),
        P("row", "col"),
        P(("dp", "col"), None),
        P(("dp", "row"), None),
    )
    return jax.shard_map(
        local, mesh=mesh, in_specs=in_specs, out_specs=P("dp", None), check_vma=False
    )
```

```python
import jax
import jax.numpy as jnp
from jax import lax
from jax.experimental import pallas as pl
from jax.experimental.pallas import tpu as pltpu
from jax.sharding import PartitionSpec as P

DG = 28672
DA = 8192
RANK = 32
NQ = 4
TOK = 512
DAMP_RATIO = 0.1

NX = 4
NZ = 8
KB = 3584
KH = KB // 2
IB = 896
LB = 512
JB = 512
PW = 768
QW = KH - PW
TILE = 256
ROWS = 128
ORDER = (0, -1, 1, -2, 2, -3, 3, 4)

BF = jnp.bfloat16
F32 = jnp.float32
MESH = pl.DeviceIdType.MESH


def plane_scratch(tag, rows, kind):
    eighth, quarter = rows // 8, rows // 4
    V = pltpu.VMEM
    return {
        tag + "csp": V((2, rows, PW), kind),
        tag + "csq": V((2, rows, QW), kind),
        tag + "crp": V((2, rows, PW), kind),
        tag + "crq": V((2, rows, QW), kind),
        tag + "owp": V((2, rows, PW), F32),
        tag + "owq": V((2, rows, QW), F32),
        tag + "ps": V((2, rows, PW), kind),
        tag + "qs": V((2, 2, NX, eighth, QW), kind),
        tag + "pr": V((2, 3, quarter, PW), kind),
        tag + "qr": V((3, NX, eighth, QW), kind),
        tag + "p2": V((2, 2, eighth, PW), kind),
        tag + "p2f": V((2, 2, eighth, PW), F32),
        tag + "q2": V((NX, eighth, QW), kind),
        tag + "q2f": V((NX, eighth, QW), F32),
        tag + "pr2": V((3, eighth, PW), kind),
        tag + "qr2": V((3, eighth, QW), kind),
        tag + "f": V((2 * rows, KH), BF) if rows >= 128 else V((16, 16, KH // 2), BF),
    }


def scratch():
    V = pltpu.VMEM
    shapes = {
        "x": V((2, 2 * ROWS, IB), BF),
        "b": V((IB, KB), BF),
        "bin": V((JB, LB), BF),
        "eig": V((KH, LB), BF),
        "ql": V((IB, 128), BF),
        "qr": V((JB, 128), BF),
        "qlt": V((128, IB), BF),
        "y": V((8, 2, 32, JB), BF),
        "qrt": V((128, JB), BF),
        "rs": V((8, 16, 256), F32),
        "rr": V((8, 16, 256), F32),
        "ro": V((8, 16, 256), F32),
        "rzr": V((7, 16, 256), F32),
        "rfin": V((2, 8, 16, 256), BF),
        "ads": V((8, 64, 256), BF),
        "adr": V((8, 64, 256), BF),
        "ao": V((8, 64, 256), F32),
        "azs": V((8, 64, 256), BF),
        "azr": V((7, 64, 256), BF),
        "afin": V((2, 8, 64, 256), BF),
        "rm": V((NQ, 128, LB), BF),
        "lt": V((KH, 128), BF),
        "pq": V((NQ, KH, LB), BF),
        "at": V((2 * ROWS, LB), F32),
        "mc": V((2 * ROWS, 128), F32),
        "m": V((TOK, 128), F32),
        "dmp": V((4, 8, 128), F32),
        "dmz": V((7, 8, 128), F32),
        "dmx": V((3, 8, 128), F32),
        "dmy": V((3, 8, 128), F32),
        "dmc": V((8, 128), F32),
        "fcs": V((2, 8, 128), F32),
        "fzr": V((15, 8, 128), F32),
        "fps": V((8, 128), F32),
        "fpr": V((15, 8, 128), F32),
        "fin": V((2, 8, 128), F32),
    }
    shapes.update(plane_scratch("l_", 64, F32))
    shapes.update(plane_scratch("a_", ROWS, BF))
    shapes.update(plane_scratch("b_", ROWS, BF))
    return shapes


N_SEM = 176
NAMES = tuple(scratch())


def kernel(xg, yg, b_hbm, bin_hbm, eig_hbm, ql_hbm, qr_hbm, out_ref, *refs):
    s = dict(zip(NAMES, refs))
    send_sems, recv_sems, local_sems = refs[len(NAMES) :]
    d = lax.axis_index("dp")
    r = lax.axis_index("row")
    c = lax.axis_index("col")
    x = c // 4
    yl = lax.rem(c // 2, 2)
    e = lax.rem(c, 2)

    def dev(dp=None, z=None, xx=None, yy=None, ee=None):
        dp = d if dp is None else dp
        z = r if z is None else z
        xx = x if xx is None else xx
        yy = yl if yy is None else yy
        ee = e if ee is None else ee
        return {"dp": dp, "row": z, "col": xx * 4 + yy * 2 + ee}

    def zp(off):
        return lax.rem(r + off, NZ)

    def xp(off):
        return lax.rem(x + off, NX)

    y_peers = ((1 - d, yl), (1 - d, 1 - yl), (d, 1 - yl))

    started = []
    local_started = []

    def send(src, dst, device):
        k = len(started)
        copy = pltpu.make_async_remote_copy(
            src_ref=src,
            dst_ref=dst,
            send_sem=send_sems.at[k],
            recv_sem=recv_sems.at[k],
            device_id=device,
            device_id_type=MESH,
        )
        copy.start()
        started.append(copy)
        return copy

    def fetch(src, dst):
        copy = pltpu.make_async_copy(src, dst, local_sems.at[len(local_started)])
        copy.start()
        local_started.append(copy)
        return copy

    def got(copies):
        for copy in copies:
            copy.wait_recv()

    def aligned(value, step):
        return pl.multiple_of(value, step)

    get_b = fetch(b_hbm, s["b"])
    get_ql = fetch(ql_hbm, s["ql"])
    get_qr = fetch(qr_hbm, s["qr"])
    get_bin = fetch(bin_hbm, s["bin"])
    get_eig = fetch(eig_hbm.at[pl.ds(aligned(d * KH, 256), KH)], s["eig"])

    def place(rel, part=None):
        position = ORDER.index(rel)
        base = lax.rem(position % 4 + 2 * e, 4) * 64
        if part is None:
            return s["x"].at[position // 4, pl.ds(aligned(base, 64), 64)]
        return s["x"].at[position // 4, pl.ds(aligned(base + part * 32, 32), 32)]

    get_x = fetch(xg, place(0))
    get_y = fetch(yg, s["y"].at[x * 2 + yl, e])

    barrier = pltpu.get_barrier_semaphore()
    peers = [dev(z=zp(off)) for off in range(1, NZ)]
    for off in range(NX):
        for dp, yy in ((d, yl),) + y_peers:
            if off or dp is not d or yy is not yl:
                peers.append(dev(dp=dp, xx=xp(off), yy=yy))
    peers += [dev(z=zp(off), ee=1 - e) for off in range(NZ)]
    for peer in peers:
        pl.semaphore_signal(barrier, inc=1, device_id=peer, device_id_type=MESH)
    partner = dev(ee=1 - e)

    def partial_group(tag, rows, lhs, h, q_group):
        width = QW if q_group else PW
        own, out = (s[tag + "owq"], s[tag + "csq"]) if q_group else (s[tag + "owp"], s[tag + "csp"])
        landing = s[tag + "crq"] if q_group else s[tag + "crp"]
        base = h * KH + (PW if q_group else 0)

        def tile(j, carry):
            columns = pl.ds(aligned(base + j * TILE, 128), TILE)
            part = jnp.dot(lhs[...], s["b"][:, columns], preferred_element_type=F32)
            here = pl.ds(aligned(j * TILE, TILE), TILE)
            own[h, :, here] = part[:rows]
            out[h, :, here] = part[rows:].astype(out.dtype)
            return carry

        lax.fori_loop(0, width // TILE, tile, 0)
        return lambda: send(out.at[h], landing.at[h], partner)

    def chip_sum(tag, rows, h, q_group):
        eighth = rows // 8
        own = s[tag + "owq"] if q_group else s[tag + "owp"]
        landing = s[tag + "crq"] if q_group else s[tag + "crp"]
        out = s[tag + "qs"] if q_group else s[tag + "ps"]

        def chunk(i, carry):
            here = pl.ds(aligned(i * eighth, eighth), eighth)
            total = own[h, here, :] + landing[h, here, :].astype(F32)
            own[h, here, :] = total
            if q_group:
                out[h, lax.rem(i, 2), i // 2] = total.astype(out.dtype)
            else:
                out[h, here, :] = total.astype(out.dtype)
            return carry

        lax.fori_loop(0, 8, chunk, 0)

    def first_p(tag, rows, h, slot_h):
        quarter = rows // 4
        return [
            send(
                s[tag + "ps"].at[h, pl.ds(aligned(xp(off) * quarter, quarter), quarter)],
                s[tag + "pr"].at[h, off - 1],
                dev(xx=xp(off)),
            )
            for off in range(1, NX)
        ]

    def first_q(tag, which):
        return [
            send(s[tag + "qs"].at[dp, yy], s[tag + "qr"].at[i], dev(dp=dp, yy=yy))
            for i, (dp, yy) in enumerate(y_peers)
            if i in which
        ]

    def second_p(tag, rows, h, which):
        eighth, quarter = rows // 8, rows // 4
        for yy in range(2):
            here = pl.ds(aligned(x * quarter + yy * eighth, eighth), eighth)
            total = s[tag + "owp"][h, here, :]
            for i in range(3):
                total += s[tag + "pr"][h, i, yy * eighth : (yy + 1) * eighth, :].astype(F32)
            s[tag + "p2f"][h, yy] = total
            s[tag + "p2"][h, yy] = total.astype(s[tag + "p2"].dtype)
        return [
            send(s[tag + "p2"].at[dp, yy], s[tag + "pr2"].at[i], dev(dp=dp, yy=yy))
            for i, (dp, yy) in enumerate(y_peers)
            if i in which
        ]

    def second_q(tag, rows):
        eighth, quarter = rows // 8, rows // 4
        for xx in range(NX):
            here = pl.ds(aligned(xx * quarter + yl * eighth, eighth), eighth)
            total = s[tag + "owq"][d, here, :]
            for i in range(3):
                total += s[tag + "qr"][i, xx].astype(F32)
            s[tag + "q2f"][xx] = total
            s[tag + "q2"][xx] = total.astype(s[tag + "q2"].dtype)
        return [
            send(s[tag + "q2"].at[xp(off)], s[tag + "qr2"].at[off - 1], dev(xx=xp(off)))
            for off in range(1, NX)
        ]

    def last_sum(tag, rows):
        eighth, quarter = rows // 8, rows // 4
        here = pl.ds(aligned(e * rows + x * quarter + yl * eighth, eighth), eighth)
        p_total = s[tag + "p2f"][d, yl]
        q_total = s[tag + "q2f"][x]
        for i in range(3):
            p_total += s[tag + "pr2"][i].astype(F32)
            q_total += s[tag + "qr2"][i].astype(F32)
        if rows >= 128:
            s[tag + "f"][here, :PW] = p_total.astype(BF)
            s[tag + "f"][here, PW:] = q_total.astype(BF)
            block = s[tag + "f"].at[here]
        else:
            whole = jnp.concatenate([p_total, q_total], axis=1)
            halves = [whole[:, : KH // 2], whole[:, KH // 2 :]]
            s[tag + "f"][e * 8 + x * 2 + yl] = jnp.concatenate(halves, axis=0).astype(BF)
            block = s[tag + "f"].at[e * 8 + x * 2 + yl]
        copies = []
        for off in range(NX):
            for yy in (yl, 1 - yl):
                if off or yy is not yl:
                    copies.append(send(block, block, dev(xx=xp(off), yy=yy)))
        return copies

    def to_partner(tag, rows):
        count = rows if rows >= 128 else 8
        block = s[tag + "f"].at[pl.ds(aligned(e * count, count), count)]
        return [send(block, block, partner)]

    groups = ((1 - d, True), (1 - d, False), (d, True), (d, False))

    get_ql.wait()
    turned = s["ql"][...].astype(F32).T.astype(BF)
    s["qlt"][:64] = jnp.where(e == 0, turned[:64], turned[64:])
    s["qlt"][64:] = jnp.where(e == 0, turned[64:], turned[:64])
    get_qr.wait()
    s["qrt"][...] = s["qr"][...].astype(F32).T.astype(BF)
    pl.semaphore_wait(barrier, len(peers))

    z_near = [
        send(xg, place(-1), dev(z=zp(1))),
        send(xg, place(1), dev(z=zp(NZ - 1))),
        send(xg, place(-2), dev(z=zp(2))),
    ]
    z_far = [send(xg, place(2), dev(z=zp(NZ - 2)))]
    mine = s["y"].at[x * 2 + yl, e]
    y_in = []
    for off in range(NX):
        for yy in (yl, 1 - yl):
            if off or yy is not yl:
                y_in.append(send(yg, mine, dev(xx=xp(off), yy=yy)))

    def half_columns(half):
        return pl.ds(aligned(half * 256, 256), 256)

    get_bin.wait()
    factor_part = jnp.dot(s["qrt"][...], s["bin"][:, half_columns(1 - d)], preferred_element_type=F32)
    s["rs"][...] = factor_part.reshape(8, 16, 256)
    r_dp = [send(s["rs"], s["rr"], dev(dp=1 - d))]
    factor_part = jnp.dot(s["qrt"][...], s["bin"][:, half_columns(d)], preferred_element_type=F32)
    s["ro"][...] = factor_part.reshape(8, 16, 256)

    get_b.wait()
    l_core = [partial_group("l_", 64, s["qlt"], h, q)() for h, q in groups]

    def first_steps(tag, rows, core_copies, i):
        h, q_group = groups[i]
        got([core_copies[i]])
        chip_sum(tag, rows, h, q_group)
        if q_group:
            return first_q(tag, (0, 1) if i == 0 else (2,))
        return first_p(tag, rows, h, i)

    l_first = [first_steps("l_", 64, l_core, i) for i in range(4)]
    got(y_in)
    get_y.wait()
    y_half = s["y"].at[:, e]
    y_core = [send(y_half, y_half, partner)]

    got(y_core)
    token_part = jnp.dot(
        s["y"][...].reshape(TOK, JB), s["bin"][:, half_columns(1 - d)], preferred_element_type=F32
    )
    s["ads"][...] = token_part.reshape(8, 64, 256).astype(BF)
    a_dp = [send(s["ads"], s["adr"], dev(dp=1 - d))]
    token_part = jnp.dot(
        s["y"][...].reshape(TOK, JB), s["bin"][:, half_columns(d)], preferred_element_type=F32
    )
    s["ao"][...] = token_part.reshape(8, 64, 256)

    got(z_near)
    z_next = [
        send(place(-2), place(-3), dev(z=zp(1))),
        send(place(-2, 0), place(4, 0), dev(z=zp(2))),
    ]
    got(z_far)
    z_next += [
        send(place(2), place(3), dev(z=zp(NZ - 1))),
        send(place(2, 1), place(4, 1), dev(z=zp(NZ - 2))),
    ]
    get_x.wait()

    a_core, a_first_in = [], []
    for i in range(4):
        a_core.append(partial_group("a_", ROWS, s["x"].at[0], *groups[i])())
        if i:
            a_first_in.append(first_steps("a_", ROWS, a_core, i - 1))
    a_first_in.append(first_steps("a_", ROWS, a_core, 3))
    get_eig.wait()

    def eig_sum(i, total):
        rows = s["eig"][pl.ds(aligned(i * 128, 128), 128), :].astype(F32)
        return total + jnp.sum(rows.reshape(16, 8, LB), axis=0)

    total = lax.fori_loop(0, KH // 128, eig_sum, jnp.zeros((8, LB), F32))
    s["dmp"][0] = total[:, :128] + total[:, 128:256] + total[:, 256:384] + total[:, 384:]
    dm_z = [send(s["dmp"].at[0], s["dmz"].at[off - 1], dev(z=zp(off))) for off in range(1, NZ)]

    got(r_dp)
    s["ro"][...] += s["rr"][...]
    r_z = [send(s["ro"].at[zp(off)], s["rzr"].at[off - 1], dev(z=zp(off))) for off in range(1, NZ)]

    got(a_dp)
    summed = s["ao"][...] + s["adr"][...].astype(F32)
    s["ao"][...] = summed
    s["azs"][...] = summed.astype(BF)
    a_z = [send(s["azs"].at[zp(off)], s["azr"].at[off - 1], dev(z=zp(off))) for off in range(1, NZ)]

    def second_steps(tag, rows, first):
        got(first[0])
        got(first[2])
        copies = second_q(tag, rows)
        got(first[1])
        copies += second_p(tag, rows, 1 - d, (0, 1))
        got(first[3])
        return copies + second_p(tag, rows, d, (2,))

    l_second = second_steps("l_", 64, l_first)

    got(z_next)
    b_core, b_first_in = [], []
    for i in range(4):
        b_core.append(partial_group("b_", ROWS, s["x"].at[1], *groups[i])())
        if i:
            b_first_in.append(first_steps("b_", ROWS, b_core, i - 1))
    b_first_in.append(first_steps("b_", ROWS, b_core, 3))

    got(dm_z)
    s["dmp"][1] = s["dmp"][0] + jnp.sum(s["dmz"][...], axis=0)
    dm_x = [send(s["dmp"].at[1], s["dmx"].at[off - 1], dev(xx=xp(off))) for off in range(1, NX)]

    got(r_z)
    factors = s["ro"][r] + jnp.sum(s["rzr"][...], axis=0)
    s["rfin"][d, r] = factors.astype(BF)
    mine = s["rfin"].at[d, r]
    r_f = [send(mine, mine, dev(z=zp(off))) for off in range(1, NZ)]

    got(l_second)
    l_f = last_sum("l_", 64)

    a_second = second_steps("a_", ROWS, a_first_in)

    got(dm_x)
    s["dmp"][2] = s["dmp"][1] + jnp.sum(s["dmx"][...], axis=0)
    dm_y = [
        send(s["dmp"].at[2], s["dmy"].at[i], dev(dp=dp, yy=yy)) for i, (dp, yy) in enumerate(y_peers)
    ]

    got(a_z)
    summed = s["ao"][r]
    for i in range(7):
        summed += s["azr"][i].astype(F32)
    s["afin"][d, r] = summed.astype(BF)
    mine = s["afin"].at[d, r]
    a_f = [send(mine, mine, dev(z=zp(off))) for off in range(1, NZ)]

    got(r_f)
    mine = s["rfin"].at[d]
    r_last = [send(mine, mine, dev(dp=1 - d))]
    got(l_f)
    l_last = to_partner("l_", 64)

    got(a_second)
    a_out = last_sum("a_", ROWS)

    got(dm_y)
    s["dmp"][3] = s["dmp"][2] + jnp.sum(s["dmy"][...], axis=0)
    dm_c = [send(s["dmp"].at[3], s["dmc"], partner)]
    b_second = second_steps("b_", ROWS, b_first_in)

    got(dm_c)
    damping = jnp.sum(s["dmp"][3] + s["dmc"][...], keepdims=True) * (DAMP_RATIO / (DG * DA))
    got(l_last)
    for i in range(2):
        left_rows = s["l_f"][...].astype(F32)[:, i * 8 : (i + 1) * 8].reshape(128, KH // 2)
        s["lt"][i * (KH // 2) : (i + 1) * (KH // 2)] = left_rows.T.astype(BF)
    got(r_last)
    for q in range(NQ):
        s["rm"][q] = jnp.zeros((128, LB), BF)
        for g in range(2):
            rows = slice(q * RANK + g * 16, q * RANK + (g + 1) * 16)
            for half in range(2):
                s["rm"][q, rows, half * 256 : (half + 1) * 256] = s["rfin"][half, q * 2 + g]

    def precondition(i, carry):
        rows = pl.ds(aligned(i * 128, 128), 128)
        inverse = 1.0 / (s["eig"][rows, :].astype(F32) + damping)
        left_rows = s["lt"][rows, :]
        for q in range(NQ):
            product = jnp.dot(left_rows, s["rm"][q], preferred_element_type=F32)
            s["pq"][q, rows, :] = (product * inverse).astype(BF)
        return carry

    lax.fori_loop(0, KH // 128, precondition, 0)

    got(b_second)
    b_out = last_sum("b_", ROWS)

    got(a_f)
    mine = s["afin"].at[d]
    a_last = [send(mine, mine, dev(dp=1 - d))]

    got(a_out)
    a_both = to_partner("a_", ROWS)
    got(a_last)

    lanes = lax.broadcasted_iota(jnp.int32, (2 * ROWS, 128), 1)
    block_of = lax.broadcasted_iota(jnp.int32, (2 * ROWS, 128), 0) // 64

    def score(tag, chunk):
        blocks = [lax.rem(r + ORDER[chunk * 4 + j] + NZ, NZ) for j in range(4)]
        odd = jnp.zeros_like(lanes)
        for j, block in enumerate(blocks):
            odd = jnp.where(block_of == j, lax.rem(block // 2, 2), odd)
            for half in range(2):
                columns = slice(half * 256, (half + 1) * 256)
                s["at"][j * 64 : (j + 1) * 64, columns] = s["afin"][half, block].astype(F32)
        s["mc"][...] = jnp.zeros((2 * ROWS, 128), F32)

        def one_query(q, carry):
            weighted = jnp.dot(s[tag + "f"][...], s["pq"][q], preferred_element_type=F32)
            terms = weighted * s["at"][...]
            total = terms[:, :128] + terms[:, 128:256] + terms[:, 256:384] + terms[:, 384:]
            scores = jnp.sum(total, axis=1, keepdims=True)
            s["mc"][...] += jnp.where(lanes == q + 4 * odd, scores, 0.0)
            return carry

        lax.fori_loop(0, NQ, one_query, 0)
        for j, block in enumerate(blocks):
            s["m"][pl.ds(aligned(block * 64, 64), 64), :] = s["mc"][j * 64 : (j + 1) * 64, :]

    got(a_both)
    score("a_", 0)
    drained = len(started)
    for copy in started[: drained - 9]:
        copy.wait_send()
    got(b_out)
    b_both = to_partner("b_", ROWS)
    got(b_both)
    score("b_", 1)

    turned = s["m"][...].T[:8]
    for half in range(2):
        base = half * 256
        s["fcs"][half] = turned[:, base : base + 128] + turned[:, base + 128 : base + 256]
    f_z = []
    for off in range(NZ):
        for ee in (e, 1 - e):
            if off or ee is not e:
                f_z.append(send(s["fcs"].at[ee], s["fzr"].at[len(f_z)], dev(z=zp(off), ee=ee)))
    got(f_z)
    s["fps"][...] = s["fcs"][e] + jnp.sum(s["fzr"][...], axis=0)
    f_plane = []
    for off in range(NX):
        for dp, yy in ((d, yl),) + y_peers:
            if off or dp is not d or yy is not yl:
                f_plane.append(send(s["fps"], s["fpr"].at[len(f_plane)], dev(dp=dp, xx=xp(off), yy=yy)))
    got(f_plane)
    s["fin"][e] = s["fps"][...] + jnp.sum(s["fpr"][...], axis=0)
    mine = s["fin"].at[e]
    f_last = [send(mine, mine, partner)]
    got(f_last)
    for half in range(2):
        for part in range(2):
            columns = slice((half * 2 + part) * 128, (half * 2 + part + 1) * 128)
            low = s["fin"][half, part * 4 : part * 4 + 2, :]
            high = s["fin"][half, part * 4 + 2 : part * 4 + 4, :]
            out_ref[:, columns] = jnp.where(d == 0, low, high)

    for copy in started[drained - 9 :]:
        copy.wait_send()


def local(out_grads, layer_inputs, basis_output, basis_input, eigenvalues, query_left, query_right):
    any_space = pl.BlockSpec(memory_space=pl.ANY)
    return pl.pallas_call(
        kernel,
        out_shape=jax.ShapeDtypeStruct((2, TOK), F32),
        in_specs=[any_space] * 7,
        out_specs=pl.BlockSpec(memory_space=pltpu.VMEM),
        scratch_shapes=list(scratch().values())
        + [
            pltpu.SemaphoreType.DMA((N_SEM,)),
            pltpu.SemaphoreType.DMA((N_SEM,)),
            pltpu.SemaphoreType.DMA((8,)),
        ],
        compiler_params=pltpu.CompilerParams(
            collective_id=0, has_side_effects=True, vmem_limit_bytes=60 * 1024 * 1024
        ),
        cost_estimate=pl.CostEstimate(flops=9_000_000_000, bytes_accessed=11_000_000, transcendentals=0),
    )(out_grads, layer_inputs, basis_output, basis_input, eigenvalues, query_left, query_right)


def solution(mesh):
    in_specs = (
        P("row", ("dp", "col")),
        P("col", ("dp", "row")),
        P(("dp", "col"), "row"),
        P(("dp", "row"), "col"),
        P("row", "col"),
        P(("dp", "col"), None),
        P(("dp", "row"), None),
    )
    return jax.shard_map(
        local, mesh=mesh, in_specs=in_specs, out_specs=P("dp", None), check_vma=False
    )
```

```python
import jax
import jax.numpy as jnp
from jax import lax
from jax.experimental import pallas as pl
from jax.experimental.pallas import tpu as pltpu
from jax.sharding import PartitionSpec as P

DG = 28672
DA = 8192
RANK = 32
NQ = 4
TOK = 512
DAMP_RATIO = 0.1

NX = 4
NZ = 8
KB = 3584
KH = KB // 2
IB = 896
LB = 512
JB = 512
PW = 1024
QW = KH - PW
TILE = 256
ROWS = 128
ORDER = (0, -1, 1, -2, 2, -3, 3, 4)

BF = jnp.bfloat16
F32 = jnp.float32
MESH = pl.DeviceIdType.MESH


def plane_scratch(tag, rows, kind):
    eighth, quarter = rows // 8, rows // 4
    V = pltpu.VMEM
    return {
        tag + "csp": V((2, rows, PW), kind),
        tag + "csq": V((2, rows, QW), kind),
        tag + "crp": V((2, rows, PW), kind),
        tag + "crq": V((2, rows, QW), kind),
        tag + "owp": V((2, rows, PW), F32),
        tag + "owq": V((2, rows, QW), F32),
        tag + "ps": V((2, rows, PW), kind),
        tag + "qs": V((2, 2, NX, eighth, QW), kind),
        tag + "pr": V((2, 3, quarter, PW), kind),
        tag + "qr": V((3, NX, eighth, QW), kind),
        tag + "p2": V((2, 2, eighth, PW), kind),
        tag + "p2f": V((2, 2, eighth, PW), F32),
        tag + "q2": V((NX, eighth, QW), kind),
        tag + "q2f": V((NX, eighth, QW), F32),
        tag + "pr2": V((3, eighth, PW), kind),
        tag + "qr2": V((3, eighth, QW), kind),
        tag + "f": V((2 * rows, KH), BF) if rows >= 128 else V((16, 16, KH // 2), BF),
    }


def scratch():
    V = pltpu.VMEM
    shapes = {
        "x": V((2, 2 * ROWS, IB), BF),
        "b": V((IB, KB), BF),
        "bin": V((JB, LB), BF),
        "eig": V((KH, LB), BF),
        "ql": V((IB, 128), BF),
        "qr": V((JB, 128), BF),
        "qlt": V((128, IB), BF),
        "y": V((8, 2, 32, JB), BF),
        "qrt": V((128, JB), BF),
        "rs": V((8, 16, 256), F32),
        "rr": V((8, 16, 256), F32),
        "ro": V((8, 16, 256), F32),
        "rzr": V((7, 16, 256), F32),
        "rfin": V((8, 2, 16, 256), BF),
        "ao": V((8, 64, LB), F32),
        "azs": V((8, 64, LB), BF),
        "azr": V((7, 64, LB), BF),
        "ads": V((64, LB), BF),
        "adr": V((64, LB), BF),
        "asum": V((64, LB), F32),
        "afin": V((8, 64, LB), BF),
        "rm": V((NQ, 128, LB), BF),
        "lt": V((KH, 128), BF),
        "pq": V((NQ, KH, LB), BF),
        "at": V((2 * ROWS, LB), F32),
        "mc": V((2 * ROWS, 128), F32),
        "m": V((TOK, 128), F32),
        "dmp": V((4, 8, 128), F32),
        "dmz": V((7, 8, 128), F32),
        "dmx": V((3, 8, 128), F32),
        "dmy": V((3, 8, 128), F32),
        "dmc": V((8, 128), F32),
        "fcs": V((2, 8, 128), F32),
        "fzr": V((15, 8, 128), F32),
        "fps": V((8, 128), F32),
        "fpr": V((15, 8, 128), F32),
        "fin": V((2, 8, 128), F32),
    }
    shapes.update(plane_scratch("l_", 64, F32))
    shapes.update(plane_scratch("a_", ROWS, BF))
    shapes.update(plane_scratch("b_", ROWS, BF))
    return shapes


N_SEM = 176
NAMES = tuple(scratch())


def kernel(xg, yg, b_hbm, bin_hbm, eig_hbm, ql_hbm, qr_hbm, out_ref, *refs):
    s = dict(zip(NAMES, refs))
    send_sems, recv_sems, local_sems = refs[len(NAMES) :]
    d = lax.axis_index("dp")
    r = lax.axis_index("row")
    c = lax.axis_index("col")
    x = c // 4
    yl = lax.rem(c // 2, 2)
    e = lax.rem(c, 2)

    def dev(dp=None, z=None, xx=None, yy=None, ee=None):
        dp = d if dp is None else dp
        z = r if z is None else z
        xx = x if xx is None else xx
        yy = yl if yy is None else yy
        ee = e if ee is None else ee
        return {"dp": dp, "row": z, "col": xx * 4 + yy * 2 + ee}

    def zp(off):
        return lax.rem(r + off, NZ)

    def xp(off):
        return lax.rem(x + off, NX)

    y_peers = ((1 - d, yl), (1 - d, 1 - yl), (d, 1 - yl))

    started = []
    local_started = []

    def send(src, dst, device):
        k = len(started)
        copy = pltpu.make_async_remote_copy(
            src_ref=src,
            dst_ref=dst,
            send_sem=send_sems.at[k],
            recv_sem=recv_sems.at[k],
            device_id=device,
            device_id_type=MESH,
        )
        copy.start()
        started.append(copy)
        return copy

    def fetch(src, dst):
        copy = pltpu.make_async_copy(src, dst, local_sems.at[len(local_started)])
        copy.start()
        local_started.append(copy)
        return copy

    def got(copies):
        for copy in copies:
            copy.wait_recv()

    def aligned(value, step):
        return pl.multiple_of(value, step)

    get_b = fetch(b_hbm, s["b"])
    get_ql = fetch(ql_hbm, s["ql"])
    get_qr = fetch(qr_hbm, s["qr"])
    get_bin = fetch(bin_hbm, s["bin"])
    get_eig = fetch(eig_hbm.at[pl.ds(aligned(d * KH, 256), KH)], s["eig"])

    def place(rel, part=None):
        position = ORDER.index(rel)
        base = lax.rem(position % 4 + 2 * e, 4) * 64
        if part is None:
            return s["x"].at[position // 4, pl.ds(aligned(base, 64), 64)]
        return s["x"].at[position // 4, pl.ds(aligned(base + part * 32, 32), 32)]

    get_x = fetch(xg, place(0))
    get_y = fetch(yg, s["y"].at[x * 2 + yl, e])

    barrier = pltpu.get_barrier_semaphore()
    peers = [dev(z=zp(off)) for off in range(1, NZ)]
    for off in range(NX):
        for dp, yy in ((d, yl),) + y_peers:
            if off or dp is not d or yy is not yl:
                peers.append(dev(dp=dp, xx=xp(off), yy=yy))
    peers += [dev(z=zp(off), ee=1 - e) for off in range(NZ)]
    for peer in peers:
        pl.semaphore_signal(barrier, inc=1, device_id=peer, device_id_type=MESH)
    partner = dev(ee=1 - e)

    def partial_group(tag, rows, lhs, h, q_group):
        width = QW if q_group else PW
        own, out = (s[tag + "owq"], s[tag + "csq"]) if q_group else (s[tag + "owp"], s[tag + "csp"])
        landing = s[tag + "crq"] if q_group else s[tag + "crp"]
        base = h * KH + (PW if q_group else 0)

        def tile(j, carry):
            columns = pl.ds(aligned(base + j * TILE, 128), TILE)
            part = jnp.dot(lhs[...], s["b"][:, columns], preferred_element_type=F32)
            here = pl.ds(aligned(j * TILE, TILE), TILE)
            own[h, :, here] = part[:rows]
            out[h, :, here] = part[rows:].astype(out.dtype)
            return carry

        lax.fori_loop(0, width // TILE, tile, 0)
        return lambda: send(out.at[h], landing.at[h], partner)

    def chip_sum(tag, rows, h, q_group):
        eighth = rows // 8
        own = s[tag + "owq"] if q_group else s[tag + "owp"]
        landing = s[tag + "crq"] if q_group else s[tag + "crp"]
        out = s[tag + "qs"] if q_group else s[tag + "ps"]

        def chunk(i, carry):
            here = pl.ds(aligned(i * eighth, eighth), eighth)
            total = own[h, here, :] + landing[h, here, :].astype(F32)
            own[h, here, :] = total
            if q_group:
                out[h, lax.rem(i, 2), i // 2] = total.astype(out.dtype)
            else:
                out[h, here, :] = total.astype(out.dtype)
            return carry

        lax.fori_loop(0, 8, chunk, 0)

    def first_p(tag, rows, h, slot_h):
        quarter = rows // 4
        return [
            send(
                s[tag + "ps"].at[h, pl.ds(aligned(xp(off) * quarter, quarter), quarter)],
                s[tag + "pr"].at[h, off - 1],
                dev(xx=xp(off)),
            )
            for off in range(1, NX)
        ]

    def first_q(tag, which):
        return [
            send(s[tag + "qs"].at[dp, yy], s[tag + "qr"].at[i], dev(dp=dp, yy=yy))
            for i, (dp, yy) in enumerate(y_peers)
            if i in which
        ]

    def second_p(tag, rows, h, which):
        eighth, quarter = rows // 8, rows // 4
        for yy in range(2):
            here = pl.ds(aligned(x * quarter + yy * eighth, eighth), eighth)
            total = s[tag + "owp"][h, here, :]
            for i in range(3):
                total += s[tag + "pr"][h, i, yy * eighth : (yy + 1) * eighth, :].astype(F32)
            s[tag + "p2f"][h, yy] = total
            s[tag + "p2"][h, yy] = total.astype(s[tag + "p2"].dtype)
        return [
            send(s[tag + "p2"].at[dp, yy], s[tag + "pr2"].at[i], dev(dp=dp, yy=yy))
            for i, (dp, yy) in enumerate(y_peers)
            if i in which
        ]

    def second_q(tag, rows):
        eighth, quarter = rows // 8, rows // 4
        for xx in range(NX):
            here = pl.ds(aligned(xx * quarter + yl * eighth, eighth), eighth)
            total = s[tag + "owq"][d, here, :]
            for i in range(3):
                total += s[tag + "qr"][i, xx].astype(F32)
            s[tag + "q2f"][xx] = total
            s[tag + "q2"][xx] = total.astype(s[tag + "q2"].dtype)
        return [
            send(s[tag + "q2"].at[xp(off)], s[tag + "qr2"].at[off - 1], dev(xx=xp(off)))
            for off in range(1, NX)
        ]

    def last_sum(tag, rows):
        eighth, quarter = rows // 8, rows // 4
        here = pl.ds(aligned(e * rows + x * quarter + yl * eighth, eighth), eighth)
        p_total = s[tag + "p2f"][d, yl]
        q_total = s[tag + "q2f"][x]
        for i in range(3):
            p_total += s[tag + "pr2"][i].astype(F32)
            q_total += s[tag + "qr2"][i].astype(F32)
        if rows >= 128:
            s[tag + "f"][here, :PW] = p_total.astype(BF)
            s[tag + "f"][here, PW:] = q_total.astype(BF)
            block = s[tag + "f"].at[here]
        else:
            whole = jnp.concatenate([p_total, q_total], axis=1)
            halves = [whole[:, : KH // 2], whole[:, KH // 2 :]]
            s[tag + "f"][e * 8 + x * 2 + yl] = jnp.concatenate(halves, axis=0).astype(BF)
            block = s[tag + "f"].at[e * 8 + x * 2 + yl]
        copies = []
        for off in range(NX):
            for yy in (yl, 1 - yl):
                if off or yy is not yl:
                    copies.append(send(block, block, dev(xx=xp(off), yy=yy)))
        return copies

    def to_partner(tag, rows):
        count = rows if rows >= 128 else 8
        block = s[tag + "f"].at[pl.ds(aligned(e * count, count), count)]
        return [send(block, block, partner)]

    groups = ((1 - d, True), (1 - d, False), (d, True), (d, False))

    pl.semaphore_wait(barrier, len(peers))

    z_near = [
        send(xg, place(-1), dev(z=zp(1))),
        send(xg, place(1), dev(z=zp(NZ - 1))),
        send(xg, place(-2), dev(z=zp(2))),
    ]
    z_far = [send(xg, place(2), dev(z=zp(NZ - 2)))]
    mine = s["y"].at[x * 2 + yl, e]
    y_in = []
    for off in range(NX):
        for yy in (yl, 1 - yl):
            if off or yy is not yl:
                y_in.append(send(yg, mine, dev(xx=xp(off), yy=yy)))

    def half_columns(half):
        return pl.ds(aligned(half * 256, 256), 256)

    get_ql.wait()
    turned = s["ql"][...].astype(F32).T.astype(BF)
    s["qlt"][:64] = jnp.where(e == 0, turned[:64], turned[64:])
    s["qlt"][64:] = jnp.where(e == 0, turned[64:], turned[:64])
    get_qr.wait()
    s["qrt"][...] = s["qr"][...].astype(F32).T.astype(BF)
    get_bin.wait()
    factor_part = jnp.dot(s["qrt"][...], s["bin"][:, half_columns(1 - d)], preferred_element_type=F32)
    s["rs"][...] = factor_part.reshape(8, 16, 256)
    r_dp = [send(s["rs"], s["rr"], dev(dp=1 - d))]
    factor_part = jnp.dot(s["qrt"][...], s["bin"][:, half_columns(d)], preferred_element_type=F32)
    s["ro"][...] = factor_part.reshape(8, 16, 256)

    get_b.wait()
    l_core = [partial_group("l_", 64, s["qlt"], h, q)() for h, q in groups]

    def first_steps(tag, rows, core_copies, i):
        h, q_group = groups[i]
        got([core_copies[i]])
        chip_sum(tag, rows, h, q_group)
        if q_group:
            return first_q(tag, (0, 1) if i == 0 else (2,))
        return first_p(tag, rows, h, i)

    l_first = [first_steps("l_", 64, l_core, i) for i in range(4)]
    got(y_in)
    get_y.wait()
    y_half = s["y"].at[:, e]
    y_core = [send(y_half, y_half, partner)]

    got(y_core)
    token_part = jnp.dot(s["y"][...].reshape(TOK, JB), s["bin"][...], preferred_element_type=F32)
    s["ao"][...] = token_part.reshape(8, 64, LB)
    s["azs"][...] = token_part.reshape(8, 64, LB).astype(BF)
    a_z = [send(s["azs"].at[zp(off)], s["azr"].at[off - 1], dev(z=zp(off))) for off in range(1, NZ)]

    got(z_near)
    z_next = [
        send(place(-2), place(-3), dev(z=zp(1))),
        send(place(-2, 0), place(4, 0), dev(z=zp(2))),
    ]
    got(z_far)
    z_next += [
        send(place(2), place(3), dev(z=zp(NZ - 1))),
        send(place(2, 1), place(4, 1), dev(z=zp(NZ - 2))),
    ]
    get_x.wait()

    a_core, a_first_in = [], []
    for i in range(4):
        a_core.append(partial_group("a_", ROWS, s["x"].at[0], *groups[i])())
        if i:
            a_first_in.append(first_steps("a_", ROWS, a_core, i - 1))
    a_first_in.append(first_steps("a_", ROWS, a_core, 3))
    get_eig.wait()

    def eig_sum(i, total):
        rows = s["eig"][pl.ds(aligned(i * 128, 128), 128), :].astype(F32)
        return total + jnp.sum(rows.reshape(16, 8, LB), axis=0)

    total = lax.fori_loop(0, KH // 128, eig_sum, jnp.zeros((8, LB), F32))
    s["dmp"][0] = total[:, :128] + total[:, 128:256] + total[:, 256:384] + total[:, 384:]
    dm_z = [send(s["dmp"].at[0], s["dmz"].at[off - 1], dev(z=zp(off))) for off in range(1, NZ)]

    got(r_dp)
    s["ro"][...] += s["rr"][...]
    r_z = [send(s["ro"].at[zp(off)], s["rzr"].at[off - 1], dev(z=zp(off))) for off in range(1, NZ)]

    def second_steps(tag, rows, first):
        got(first[0])
        got(first[2])
        copies = second_q(tag, rows)
        got(first[1])
        copies += second_p(tag, rows, 1 - d, (0, 1))
        got(first[3])
        return copies + second_p(tag, rows, d, (2,))

    l_second = second_steps("l_", 64, l_first)

    got(z_next)
    b_core, b_first_in = [], []
    for i in range(4):
        b_core.append(partial_group("b_", ROWS, s["x"].at[1], *groups[i])())
        if i:
            b_first_in.append(first_steps("b_", ROWS, b_core, i - 1))
    b_first_in.append(first_steps("b_", ROWS, b_core, 3))

    got(dm_z)
    s["dmp"][1] = s["dmp"][0] + jnp.sum(s["dmz"][...], axis=0)
    dm_x = [send(s["dmp"].at[1], s["dmx"].at[off - 1], dev(xx=xp(off))) for off in range(1, NX)]

    got(r_z)
    factors = s["ro"][r] + jnp.sum(s["rzr"][...], axis=0)
    s["rfin"][r, d] = factors.astype(BF)
    mine = s["rfin"].at[r, d]
    r_x = [send(mine, mine, dev(dp=1 - d))]

    got(a_z)
    summed = s["ao"][r]
    for i in range(7):
        summed += s["azr"][i].astype(F32)
    s["asum"][...] = summed
    s["ads"][...] = summed.astype(BF)
    a_dp = [send(s["ads"], s["adr"], dev(dp=1 - d))]

    got(l_second)
    l_f = last_sum("l_", 64)

    a_second = second_steps("a_", ROWS, a_first_in)

    got(dm_x)
    s["dmp"][2] = s["dmp"][1] + jnp.sum(s["dmx"][...], axis=0)
    dm_y = [
        send(s["dmp"].at[2], s["dmy"].at[i], dev(dp=dp, yy=yy)) for i, (dp, yy) in enumerate(y_peers)
    ]

    got(r_x)
    mine = s["rfin"].at[r]
    r_f = [send(mine, mine, dev(z=zp(off))) for off in range(1, NZ)]
    got(a_dp)
    s["afin"][r] = (s["asum"][...] + s["adr"][...].astype(F32)).astype(BF)
    mine = s["afin"].at[r]
    a_f = [send(mine, mine, dev(z=zp(off))) for off in range(1, NZ)]
    got(l_f)
    l_last = to_partner("l_", 64)

    got(a_second)
    a_out = last_sum("a_", ROWS)

    got(dm_y)
    s["dmp"][3] = s["dmp"][2] + jnp.sum(s["dmy"][...], axis=0)
    dm_c = [send(s["dmp"].at[3], s["dmc"], partner)]
    b_second = second_steps("b_", ROWS, b_first_in)

    got(dm_c)
    damping = jnp.sum(s["dmp"][3] + s["dmc"][...], keepdims=True) * (DAMP_RATIO / (DG * DA))
    got(l_last)
    for i in range(2):
        left_rows = s["l_f"][...].astype(F32)[:, i * 8 : (i + 1) * 8].reshape(128, KH // 2)
        s["lt"][i * (KH // 2) : (i + 1) * (KH // 2)] = left_rows.T.astype(BF)
    got(r_f)
    for q in range(NQ):
        s["rm"][q] = jnp.zeros((128, LB), BF)
        for g in range(2):
            rows = slice(q * RANK + g * 16, q * RANK + (g + 1) * 16)
            for half in range(2):
                s["rm"][q, rows, half * 256 : (half + 1) * 256] = s["rfin"][q * 2 + g, half]

    def precondition(i, carry):
        rows = pl.ds(aligned(i * 128, 128), 128)
        inverse = 1.0 / (s["eig"][rows, :].astype(F32) + damping)
        left_rows = s["lt"][rows, :]
        for q in range(NQ):
            product = jnp.dot(left_rows, s["rm"][q], preferred_element_type=F32)
            s["pq"][q, rows, :] = (product * inverse).astype(BF)
        return carry

    lax.fori_loop(0, KH // 128, precondition, 0)

    got(b_second)
    b_out = last_sum("b_", ROWS)

    got(a_out)
    a_both = to_partner("a_", ROWS)
    got(a_f)

    lanes = lax.broadcasted_iota(jnp.int32, (2 * ROWS, 128), 1)
    block_of = lax.broadcasted_iota(jnp.int32, (2 * ROWS, 128), 0) // 64

    def score(tag, chunk):
        blocks = [lax.rem(r + ORDER[chunk * 4 + j] + NZ, NZ) for j in range(4)]
        odd = jnp.zeros_like(lanes)
        for j, block in enumerate(blocks):
            odd = jnp.where(block_of == j, lax.rem(block // 2, 2), odd)
            s["at"][j * 64 : (j + 1) * 64] = s["afin"][block].astype(F32)
        s["mc"][...] = jnp.zeros((2 * ROWS, 128), F32)

        def one_query(q, carry):
            weighted = jnp.dot(s[tag + "f"][...], s["pq"][q], preferred_element_type=F32)
            terms = weighted * s["at"][...]
            total = terms[:, :128] + terms[:, 128:256] + terms[:, 256:384] + terms[:, 384:]
            scores = jnp.sum(total, axis=1, keepdims=True)
            s["mc"][...] += jnp.where(lanes == q + 4 * odd, scores, 0.0)
            return carry

        lax.fori_loop(0, NQ, one_query, 0)
        for j, block in enumerate(blocks):
            s["m"][pl.ds(aligned(block * 64, 64), 64), :] = s["mc"][j * 64 : (j + 1) * 64, :]

    got(a_both)
    score("a_", 0)
    drained = len(started)
    for copy in started[: drained - 8]:
        copy.wait_send()
    got(b_out)
    b_both = to_partner("b_", ROWS)
    got(b_both)
    score("b_", 1)

    turned = s["m"][...].T[:8]
    for half in range(2):
        base = half * 256
        s["fcs"][half] = turned[:, base : base + 128] + turned[:, base + 128 : base + 256]
    f_z = []
    for off in range(NZ):
        for ee in (e, 1 - e):
            if off or ee is not e:
                f_z.append(send(s["fcs"].at[ee], s["fzr"].at[len(f_z)], dev(z=zp(off), ee=ee)))
    got(f_z)
    s["fps"][...] = s["fcs"][e] + jnp.sum(s["fzr"][...], axis=0)
    f_plane = []
    for off in range(NX):
        for dp, yy in ((d, yl),) + y_peers:
            if off or dp is not d or yy is not yl:
                f_plane.append(send(s["fps"], s["fpr"].at[len(f_plane)], dev(dp=dp, xx=xp(off), yy=yy)))
    got(f_plane)
    s["fin"][e] = s["fps"][...] + jnp.sum(s["fpr"][...], axis=0)
    mine = s["fin"].at[e]
    f_last = [send(mine, mine, partner)]
    got(f_last)
    for half in range(2):
        for part in range(2):
            columns = slice((half * 2 + part) * 128, (half * 2 + part + 1) * 128)
            low = s["fin"][half, part * 4 : part * 4 + 2, :]
            high = s["fin"][half, part * 4 + 2 : part * 4 + 4, :]
            out_ref[:, columns] = jnp.where(d == 0, low, high)

    for copy in started[drained - 8 :]:
        copy.wait_send()


def local(out_grads, layer_inputs, basis_output, basis_input, eigenvalues, query_left, query_right):
    any_space = pl.BlockSpec(memory_space=pl.ANY)
    return pl.pallas_call(
        kernel,
        out_shape=jax.ShapeDtypeStruct((2, TOK), F32),
        in_specs=[any_space] * 7,
        out_specs=pl.BlockSpec(memory_space=pltpu.VMEM),
        scratch_shapes=list(scratch().values())
        + [
            pltpu.SemaphoreType.DMA((N_SEM,)),
            pltpu.SemaphoreType.DMA((N_SEM,)),
            pltpu.SemaphoreType.DMA((8,)),
        ],
        compiler_params=pltpu.CompilerParams(
            collective_id=0, has_side_effects=True, vmem_limit_bytes=60 * 1024 * 1024
        ),
        cost_estimate=pl.CostEstimate(flops=9_000_000_000, bytes_accessed=11_000_000, transcendentals=0),
    )(out_grads, layer_inputs, basis_output, basis_input, eigenvalues, query_left, query_right)


def solution(mesh):
    in_specs = (
        P("row", ("dp", "col")),
        P("col", ("dp", "row")),
        P(("dp", "col"), "row"),
        P(("dp", "row"), "col"),
        P("row", "col"),
        P(("dp", "col"), None),
        P(("dp", "row"), None),
    )
    return jax.shard_map(
        local, mesh=mesh, in_specs=in_specs, out_specs=P("dp", None), check_vma=False
    )
```

```python
import jax
import jax.numpy as jnp
from jax import lax
from jax.experimental import pallas as pl
from jax.experimental.pallas import tpu as pltpu
from jax.sharding import PartitionSpec as P

DG = 28672
DA = 8192
RANK = 32
NQ = 4
TOK = 512
DAMP_RATIO = 0.1

NX = 4
NZ = 8
KB = 3584
KH = KB // 2
IB = 896
LB = 512
JB = 512
PW = 1024
QW = KH - PW
TILE = 256
ROWS = 128
ORDER = (0, -1, 1, -2, 2, -3, 3, 4)

BF = jnp.bfloat16
F32 = jnp.float32
MESH = pl.DeviceIdType.MESH


def plane_scratch(tag, rows, kind):
    eighth, quarter = rows // 8, rows // 4
    V = pltpu.VMEM
    return {
        tag + "csp": V((2, rows, PW), kind),
        tag + "csq": V((2, rows, QW), kind),
        tag + "crp": V((2, rows, PW), kind),
        tag + "crq": V((2, rows, QW), kind),
        tag + "owp": V((2, rows, PW), F32),
        tag + "owq": V((2, rows, QW), F32),
        tag + "ps": V((2, rows, PW), kind),
        tag + "qs": V((2, 2, NX, eighth, QW), kind),
        tag + "pr": V((2, 3, quarter, PW), kind),
        tag + "qr": V((3, NX, eighth, QW), kind),
        tag + "p2": V((2, 2, eighth, PW), kind),
        tag + "p2f": V((2, 2, eighth, PW), F32),
        tag + "q2": V((NX, eighth, QW), kind),
        tag + "q2f": V((NX, eighth, QW), F32),
        tag + "pr2": V((3, eighth, PW), kind),
        tag + "qr2": V((3, eighth, QW), kind),
        tag + "f": V((2 * rows, KH), BF) if rows >= 128 else V((16, 16, KH // 2), BF),
    }


def scratch():
    V = pltpu.VMEM
    shapes = {
        "x": V((2, 2 * ROWS, IB), BF),
        "b": V((IB, KB), BF),
        "bin": V((JB, LB), BF),
        "eig": V((KH, LB), BF),
        "ql": V((IB, 128), BF),
        "qr": V((JB, 128), BF),
        "qlt": V((128, IB), BF),
        "y": V((8, 2, 32, JB), BF),
        "qrt": V((128, JB), BF),
        "rs": V((8, 16, 256), F32),
        "rr": V((8, 16, 256), F32),
        "ro": V((8, 16, 256), F32),
        "rzr": V((7, 16, 256), F32),
        "rfin": V((8, 2, 16, 256), BF),
        "ao": V((8, 64, 256), F32),
        "azs": V((8, 64, 256), BF),
        "azr": V((7, 64, 256), BF),
        "ads": V((8, 64, 256), BF),
        "adr": V((8, 64, 256), BF),
        "afin": V((8, 2, 64, 256), BF),
        "rm": V((NQ, 128, LB), BF),
        "lt": V((KH, 128), BF),
        "pq": V((NQ, KH, LB), BF),
        "at": V((2 * ROWS, LB), F32),
        "sv": V((2, NQ, 2 * ROWS, LB), F32),
        "mc": V((2 * ROWS, 128), F32),
        "m": V((TOK, 128), F32),
        "dmp": V((4, 8, 128), F32),
        "dmz": V((7, 8, 128), F32),
        "dmx": V((3, 8, 128), F32),
        "dmy": V((3, 8, 128), F32),
        "dmc": V((8, 128), F32),
        "fcs": V((2, 8, 128), F32),
        "fzr": V((15, 8, 128), F32),
        "fps": V((8, 128), F32),
        "fpr": V((15, 8, 128), F32),
        "fin": V((2, 8, 128), F32),
    }
    shapes.update(plane_scratch("l_", 64, F32))
    shapes.update(plane_scratch("a_", ROWS, BF))
    shapes.update(plane_scratch("b_", ROWS, BF))
    return shapes


N_SEM = 176
NAMES = tuple(scratch())


def kernel(xg, yg, b_hbm, bin_hbm, eig_hbm, ql_hbm, qr_hbm, out_ref, *refs):
    s = dict(zip(NAMES, refs))
    send_sems, recv_sems, local_sems = refs[len(NAMES) :]
    d = lax.axis_index("dp")
    r = lax.axis_index("row")
    c = lax.axis_index("col")
    x = c // 4
    yl = lax.rem(c // 2, 2)
    e = lax.rem(c, 2)

    def dev(dp=None, z=None, xx=None, yy=None, ee=None):
        dp = d if dp is None else dp
        z = r if z is None else z
        xx = x if xx is None else xx
        yy = yl if yy is None else yy
        ee = e if ee is None else ee
        return {"dp": dp, "row": z, "col": xx * 4 + yy * 2 + ee}

    def zp(off):
        return lax.rem(r + off, NZ)

    def xp(off):
        return lax.rem(x + off, NX)

    y_peers = ((1 - d, yl), (1 - d, 1 - yl), (d, 1 - yl))

    started = []
    local_started = []

    def send(src, dst, device):
        k = len(started)
        copy = pltpu.make_async_remote_copy(
            src_ref=src,
            dst_ref=dst,
            send_sem=send_sems.at[k],
            recv_sem=recv_sems.at[k],
            device_id=device,
            device_id_type=MESH,
        )
        copy.start()
        started.append(copy)
        return copy

    def fetch(src, dst):
        copy = pltpu.make_async_copy(src, dst, local_sems.at[len(local_started)])
        copy.start()
        local_started.append(copy)
        return copy

    def got(copies):
        for copy in copies:
            copy.wait_recv()

    def aligned(value, step):
        return pl.multiple_of(value, step)

    get_b = fetch(b_hbm, s["b"])
    get_ql = fetch(ql_hbm, s["ql"])
    get_qr = fetch(qr_hbm, s["qr"])
    get_bin = fetch(bin_hbm, s["bin"])
    get_eig = fetch(eig_hbm.at[pl.ds(aligned(d * KH, 256), KH)], s["eig"])

    def place(rel, part=None):
        position = ORDER.index(rel)
        base = lax.rem(position % 4 + 2 * e, 4) * 64
        if part is None:
            return s["x"].at[position // 4, pl.ds(aligned(base, 64), 64)]
        return s["x"].at[position // 4, pl.ds(aligned(base + part * 32, 32), 32)]

    get_x = fetch(xg, place(0))
    get_y = fetch(yg, s["y"].at[x * 2 + yl, e])

    barrier = pltpu.get_barrier_semaphore()
    peers = [dev(z=zp(off)) for off in range(1, NZ)]
    for off in range(NX):
        for dp, yy in ((d, yl),) + y_peers:
            if off or dp is not d or yy is not yl:
                peers.append(dev(dp=dp, xx=xp(off), yy=yy))
    peers += [dev(z=zp(off), ee=1 - e) for off in range(NZ)]
    for peer in peers:
        pl.semaphore_signal(barrier, inc=1, device_id=peer, device_id_type=MESH)
    partner = dev(ee=1 - e)

    def partial_group(tag, rows, lhs, h, q_group):
        width = QW if q_group else PW
        own, out = (s[tag + "owq"], s[tag + "csq"]) if q_group else (s[tag + "owp"], s[tag + "csp"])
        landing = s[tag + "crq"] if q_group else s[tag + "crp"]
        base = h * KH + (PW if q_group else 0)

        def tile(j, carry):
            columns = pl.ds(aligned(base + j * TILE, 128), TILE)
            part = jnp.dot(lhs[...], s["b"][:, columns], preferred_element_type=F32)
            here = pl.ds(aligned(j * TILE, TILE), TILE)
            own[h, :, here] = part[:rows]
            out[h, :, here] = part[rows:].astype(out.dtype)
            return carry

        lax.fori_loop(0, width // TILE, tile, 0)
        return lambda: send(out.at[h], landing.at[h], partner)

    def chip_sum(tag, rows, h, q_group):
        eighth = rows // 8
        own = s[tag + "owq"] if q_group else s[tag + "owp"]
        landing = s[tag + "crq"] if q_group else s[tag + "crp"]
        out = s[tag + "qs"] if q_group else s[tag + "ps"]

        def chunk(i, carry):
            here = pl.ds(aligned(i * eighth, eighth), eighth)
            total = own[h, here, :] + landing[h, here, :].astype(F32)
            own[h, here, :] = total
            if q_group:
                out[h, lax.rem(i, 2), i // 2] = total.astype(out.dtype)
            else:
                out[h, here, :] = total.astype(out.dtype)
            return carry

        lax.fori_loop(0, 8, chunk, 0)

    def first_p(tag, rows, h, slot_h):
        quarter = rows // 4
        return [
            send(
                s[tag + "ps"].at[h, pl.ds(aligned(xp(off) * quarter, quarter), quarter)],
                s[tag + "pr"].at[h, off - 1],
                dev(xx=xp(off)),
            )
            for off in range(1, NX)
        ]

    def first_q(tag, which):
        return [
            send(s[tag + "qs"].at[dp, yy], s[tag + "qr"].at[i], dev(dp=dp, yy=yy))
            for i, (dp, yy) in enumerate(y_peers)
            if i in which
        ]

    def second_p(tag, rows, h, which):
        eighth, quarter = rows // 8, rows // 4
        for yy in range(2):
            here = pl.ds(aligned(x * quarter + yy * eighth, eighth), eighth)
            total = s[tag + "owp"][h, here, :]
            for i in range(3):
                total += s[tag + "pr"][h, i, yy * eighth : (yy + 1) * eighth, :].astype(F32)
            s[tag + "p2f"][h, yy] = total
            s[tag + "p2"][h, yy] = total.astype(s[tag + "p2"].dtype)
        return [
            send(s[tag + "p2"].at[dp, yy], s[tag + "pr2"].at[i], dev(dp=dp, yy=yy))
            for i, (dp, yy) in enumerate(y_peers)
            if i in which
        ]

    def second_q(tag, rows):
        eighth, quarter = rows // 8, rows // 4
        for xx in range(NX):
            here = pl.ds(aligned(xx * quarter + yl * eighth, eighth), eighth)
            total = s[tag + "owq"][d, here, :]
            for i in range(3):
                total += s[tag + "qr"][i, xx].astype(F32)
            s[tag + "q2f"][xx] = total
            s[tag + "q2"][xx] = total.astype(s[tag + "q2"].dtype)
        return [
            send(s[tag + "q2"].at[xp(off)], s[tag + "qr2"].at[off - 1], dev(xx=xp(off)))
            for off in range(1, NX)
        ]

    def last_sum(tag, rows):
        eighth, quarter = rows // 8, rows // 4
        here = pl.ds(aligned(e * rows + x * quarter + yl * eighth, eighth), eighth)
        p_total = s[tag + "p2f"][d, yl]
        q_total = s[tag + "q2f"][x]
        for i in range(3):
            p_total += s[tag + "pr2"][i].astype(F32)
            q_total += s[tag + "qr2"][i].astype(F32)
        if rows >= 128:
            s[tag + "f"][here, :PW] = p_total.astype(BF)
            s[tag + "f"][here, PW:] = q_total.astype(BF)
            block = s[tag + "f"].at[here]
        else:
            whole = jnp.concatenate([p_total, q_total], axis=1)
            halves = [whole[:, : KH // 2], whole[:, KH // 2 :]]
            s[tag + "f"][e * 8 + x * 2 + yl] = jnp.concatenate(halves, axis=0).astype(BF)
            block = s[tag + "f"].at[e * 8 + x * 2 + yl]
        copies = []
        for off in range(NX):
            for yy in (yl, 1 - yl):
                if off or yy is not yl:
                    copies.append(send(block, block, dev(xx=xp(off), yy=yy)))
        return copies

    def to_partner(tag, rows):
        count = rows if rows >= 128 else 8
        block = s[tag + "f"].at[pl.ds(aligned(e * count, count), count)]
        return [send(block, block, partner)]

    groups = ((1 - d, True), (1 - d, False), (d, True), (d, False))

    pl.semaphore_wait(barrier, len(peers))

    z_near = [
        send(xg, place(-1), dev(z=zp(1))),
        send(xg, place(1), dev(z=zp(NZ - 1))),
        send(xg, place(-2), dev(z=zp(2))),
    ]
    z_far = [send(xg, place(2), dev(z=zp(NZ - 2)))]
    mine = s["y"].at[x * 2 + yl, e]
    y_in = []
    for off in range(NX):
        for yy in (yl, 1 - yl):
            if off or yy is not yl:
                y_in.append(send(yg, mine, dev(xx=xp(off), yy=yy)))

    def half_columns(half):
        return pl.ds(aligned(half * 256, 256), 256)

    get_ql.wait()
    turned = s["ql"][...].astype(F32).T.astype(BF)
    s["qlt"][:64] = jnp.where(e == 0, turned[:64], turned[64:])
    s["qlt"][64:] = jnp.where(e == 0, turned[64:], turned[:64])
    get_qr.wait()
    s["qrt"][...] = s["qr"][...].astype(F32).T.astype(BF)
    get_bin.wait()
    factor_part = jnp.dot(s["qrt"][...], s["bin"][:, half_columns(1 - d)], preferred_element_type=F32)
    s["rs"][...] = factor_part.reshape(8, 16, 256)
    r_dp = [send(s["rs"], s["rr"], dev(dp=1 - d))]
    factor_part = jnp.dot(s["qrt"][...], s["bin"][:, half_columns(d)], preferred_element_type=F32)
    s["ro"][...] = factor_part.reshape(8, 16, 256)

    get_b.wait()
    l_core = [partial_group("l_", 64, s["qlt"], h, q)() for h, q in groups]

    def first_steps(tag, rows, core_copies, i):
        h, q_group = groups[i]
        got([core_copies[i]])
        chip_sum(tag, rows, h, q_group)
        if q_group:
            return first_q(tag, (0, 1) if i == 0 else (2,))
        return first_p(tag, rows, h, i)

    got(y_in)
    get_y.wait()
    y_half = s["y"].at[:, e]
    y_core = [send(y_half, y_half, partner)]

    got(y_core)
    def input_part(half):
        part = jnp.dot(
            s["y"][...].reshape(TOK, JB), s["bin"][:, half_columns(half)], preferred_element_type=F32
        )
        return part.reshape(8, 64, 256)

    s["ads"][...] = input_part(1 - d).astype(BF)
    a_dp = [send(s["ads"], s["adr"], dev(dp=1 - d))]
    s["ao"][...] = input_part(d)

    l_first = [first_steps("l_", 64, l_core, i) for i in range(4)]

    got(z_near)
    z_next = [
        send(place(-2), place(-3), dev(z=zp(1))),
        send(place(-2, 0), place(4, 0), dev(z=zp(2))),
    ]
    got(z_far)
    z_next += [
        send(place(2), place(3), dev(z=zp(NZ - 1))),
        send(place(2, 1), place(4, 1), dev(z=zp(NZ - 2))),
    ]
    get_x.wait()

    a_core, a_first_in = [], []
    for i in range(4):
        a_core.append(partial_group("a_", ROWS, s["x"].at[0], *groups[i])())
        if i:
            a_first_in.append(first_steps("a_", ROWS, a_core, i - 1))
    a_first_in.append(first_steps("a_", ROWS, a_core, 3))
    got(a_dp)
    summed = s["ao"][...] + s["adr"][...].astype(F32)
    s["ao"][...] = summed
    s["azs"][...] = summed.astype(BF)
    a_z = [send(s["azs"].at[zp(off)], s["azr"].at[off - 1], dev(z=zp(off))) for off in range(1, NZ)]

    get_eig.wait()

    def eig_sum(i, total):
        rows = s["eig"][pl.ds(aligned(i * 128, 128), 128), :].astype(F32)
        return total + jnp.sum(rows.reshape(16, 8, LB), axis=0)

    total = lax.fori_loop(0, KH // 128, eig_sum, jnp.zeros((8, LB), F32))
    s["dmp"][0] = total[:, :128] + total[:, 128:256] + total[:, 256:384] + total[:, 384:]
    dm_z = [send(s["dmp"].at[0], s["dmz"].at[off - 1], dev(z=zp(off))) for off in range(1, NZ)]

    got(r_dp)
    s["ro"][...] += s["rr"][...]
    r_z = [send(s["ro"].at[zp(off)], s["rzr"].at[off - 1], dev(z=zp(off))) for off in range(1, NZ)]

    def second_steps(tag, rows, first):
        got(first[0])
        got(first[2])
        copies = second_q(tag, rows)
        got(first[1])
        copies += second_p(tag, rows, 1 - d, (0, 1))
        got(first[3])
        return copies + second_p(tag, rows, d, (2,))

    l_second = second_steps("l_", 64, l_first)

    got(z_next)
    b_core, b_first_in = [], []
    for i in range(4):
        b_core.append(partial_group("b_", ROWS, s["x"].at[1], *groups[i])())
        if i:
            b_first_in.append(first_steps("b_", ROWS, b_core, i - 1))
    b_first_in.append(first_steps("b_", ROWS, b_core, 3))

    got(dm_z)
    s["dmp"][1] = s["dmp"][0] + jnp.sum(s["dmz"][...], axis=0)
    dm_x = [send(s["dmp"].at[1], s["dmx"].at[off - 1], dev(xx=xp(off))) for off in range(1, NX)]

    got(r_z)
    factors = s["ro"][r] + jnp.sum(s["rzr"][...], axis=0)
    s["rfin"][r, d] = factors.astype(BF)
    mine = s["rfin"].at[r, d]
    r_x = [send(mine, mine, dev(dp=1 - d))]

    got(l_second)
    l_f = last_sum("l_", 64)

    a_second = second_steps("a_", ROWS, a_first_in)

    got(dm_x)
    s["dmp"][2] = s["dmp"][1] + jnp.sum(s["dmx"][...], axis=0)
    dm_y = [
        send(s["dmp"].at[2], s["dmy"].at[i], dev(dp=dp, yy=yy)) for i, (dp, yy) in enumerate(y_peers)
    ]

    got(a_z)
    summed = s["ao"][r]
    for i in range(7):
        summed += s["azr"][i].astype(F32)
    s["afin"][r, d] = summed.astype(BF)
    mine = s["afin"].at[r, d]
    a_x = [send(mine, mine, dev(dp=1 - d))]

    got(r_x)
    mine = s["rfin"].at[r]
    r_f = [send(mine, mine, dev(z=zp(off))) for off in range(1, NZ)]
    got(l_f)
    l_last = to_partner("l_", 64)

    got(a_second)
    a_out = last_sum("a_", ROWS)

    got(dm_y)
    s["dmp"][3] = s["dmp"][2] + jnp.sum(s["dmy"][...], axis=0)
    dm_c = [send(s["dmp"].at[3], s["dmc"], partner)]
    got(a_x)
    mine = s["afin"].at[r]
    a_f = [send(mine, mine, dev(z=zp(off))) for off in range(1, NZ)]
    b_second = second_steps("b_", ROWS, b_first_in)

    got(dm_c)
    damping = jnp.sum(s["dmp"][3] + s["dmc"][...], keepdims=True) * (DAMP_RATIO / (DG * DA))
    got(l_last)
    for i in range(2):
        left_rows = s["l_f"][...].astype(F32)[:, i * 8 : (i + 1) * 8].reshape(128, KH // 2)
        s["lt"][i * (KH // 2) : (i + 1) * (KH // 2)] = left_rows.T.astype(BF)
    got(r_f)
    for q in range(NQ):
        s["rm"][q] = jnp.zeros((128, LB), BF)
        for g in range(2):
            rows = slice(q * RANK + g * 16, q * RANK + (g + 1) * 16)
            for half in range(2):
                s["rm"][q, rows, half * 256 : (half + 1) * 256] = s["rfin"][q * 2 + g, half]

    def precondition(i, carry):
        rows = pl.ds(aligned(i * 128, 128), 128)
        inverse = 1.0 / (s["eig"][rows, :].astype(F32) + damping)
        left_rows = s["lt"][rows, :]
        for q in range(NQ):
            product = jnp.dot(left_rows, s["rm"][q], preferred_element_type=F32)
            s["pq"][q, rows, :] = (product * inverse).astype(BF)
        return carry

    lax.fori_loop(0, KH // 128, precondition, 0)

    got(b_second)
    b_out = last_sum("b_", ROWS)

    got(a_out)
    a_both = to_partner("a_", ROWS)

    lanes = lax.broadcasted_iota(jnp.int32, (2 * ROWS, 128), 1)
    block_of = lax.broadcasted_iota(jnp.int32, (2 * ROWS, 128), 0) // 64

    def weigh(tag, chunk):
        def one_query(q, carry):
            s["sv"][chunk, q] = jnp.dot(s[tag + "f"][...], s["pq"][q], preferred_element_type=F32)
            return carry

        lax.fori_loop(0, NQ, one_query, 0)

    def score(chunk):
        blocks = [lax.rem(r + ORDER[chunk * 4 + j] + NZ, NZ) for j in range(4)]
        odd = jnp.zeros_like(lanes)
        for j, block in enumerate(blocks):
            odd = jnp.where(block_of == j, lax.rem(block // 2, 2), odd)
            for half in range(2):
                columns = slice(half * 256, (half + 1) * 256)
                s["at"][j * 64 : (j + 1) * 64, columns] = s["afin"][block, half].astype(F32)
        s["mc"][...] = jnp.zeros((2 * ROWS, 128), F32)

        def one_query(q, carry):
            terms = s["sv"][chunk, q] * s["at"][...]
            total = terms[:, :128] + terms[:, 128:256] + terms[:, 256:384] + terms[:, 384:]
            scores = jnp.sum(total, axis=1, keepdims=True)
            s["mc"][...] += jnp.where(lanes == q + 4 * odd, scores, 0.0)
            return carry

        lax.fori_loop(0, NQ, one_query, 0)
        for j, block in enumerate(blocks):
            s["m"][pl.ds(aligned(block * 64, 64), 64), :] = s["mc"][j * 64 : (j + 1) * 64, :]

    got(a_both)
    weigh("a_", 0)
    got(b_out)
    b_both = to_partner("b_", ROWS)
    drained = len(started)
    for copy in started[: drained - 9]:
        copy.wait_send()
    got(b_both)
    weigh("b_", 1)
    got(a_f)
    score(0)
    score(1)

    turned = s["m"][...].T[:8]
    for half in range(2):
        base = half * 256
        s["fcs"][half] = turned[:, base : base + 128] + turned[:, base + 128 : base + 256]
    f_z = []
    for off in range(NZ):
        for ee in (e, 1 - e):
            if off or ee is not e:
                f_z.append(send(s["fcs"].at[ee], s["fzr"].at[len(f_z)], dev(z=zp(off), ee=ee)))
    got(f_z)
    s["fps"][...] = s["fcs"][e] + jnp.sum(s["fzr"][...], axis=0)
    f_plane = []
    for off in range(NX):
        for dp, yy in ((d, yl),) + y_peers:
            if off or dp is not d or yy is not yl:
                f_plane.append(send(s["fps"], s["fpr"].at[len(f_plane)], dev(dp=dp, xx=xp(off), yy=yy)))
    got(f_plane)
    s["fin"][e] = s["fps"][...] + jnp.sum(s["fpr"][...], axis=0)
    mine = s["fin"].at[e]
    f_last = [send(mine, mine, partner)]
    got(f_last)
    for half in range(2):
        for part in range(2):
            columns = slice((half * 2 + part) * 128, (half * 2 + part + 1) * 128)
            low = s["fin"][half, part * 4 : part * 4 + 2, :]
            high = s["fin"][half, part * 4 + 2 : part * 4 + 4, :]
            out_ref[:, columns] = jnp.where(d == 0, low, high)

    for copy in started[drained - 9 :]:
        copy.wait_send()


def local(out_grads, layer_inputs, basis_output, basis_input, eigenvalues, query_left, query_right):
    any_space = pl.BlockSpec(memory_space=pl.ANY)
    return pl.pallas_call(
        kernel,
        out_shape=jax.ShapeDtypeStruct((2, TOK), F32),
        in_specs=[any_space] * 7,
        out_specs=pl.BlockSpec(memory_space=pltpu.VMEM),
        scratch_shapes=list(scratch().values())
        + [
            pltpu.SemaphoreType.DMA((N_SEM,)),
            pltpu.SemaphoreType.DMA((N_SEM,)),
            pltpu.SemaphoreType.DMA((8,)),
        ],
        compiler_params=pltpu.CompilerParams(
            collective_id=0, has_side_effects=True, vmem_limit_bytes=60 * 1024 * 1024
        ),
        cost_estimate=pl.CostEstimate(flops=9_000_000_000, bytes_accessed=11_000_000, transcendentals=0),
    )(out_grads, layer_inputs, basis_output, basis_input, eigenvalues, query_left, query_right)


def solution(mesh):
    in_specs = (
        P("row", ("dp", "col")),
        P("col", ("dp", "row")),
        P(("dp", "col"), "row"),
        P(("dp", "row"), "col"),
        P("row", "col"),
        P(("dp", "col"), None),
        P(("dp", "row"), None),
    )
    return jax.shard_map(
        local, mesh=mesh, in_specs=in_specs, out_specs=P("dp", None), check_vma=False
    )
```

```python
import jax
import jax.numpy as jnp
from jax import lax
from jax.experimental import pallas as pl
from jax.experimental.pallas import tpu as pltpu
from jax.sharding import PartitionSpec as P

DG = 28672
DA = 8192
RANK = 32
NQ = 4
TOK = 512
DAMP_RATIO = 0.1

NX = 4
NZ = 8
KB = 3584
KH = KB // 2
IB = 896
LB = 512
JB = 512
PW = 1024
QW = KH - PW
TILE = 256
ROWS = 128
ORDER = (0, -1, 1, -2, 2, -3, 3, 4)

BF = jnp.bfloat16
F32 = jnp.float32
MESH = pl.DeviceIdType.MESH


def plane_scratch(tag, rows, kind):
    eighth, quarter = rows // 8, rows // 4
    V = pltpu.VMEM
    return {
        tag + "csp": V((2, rows, PW), kind),
        tag + "csq": V((2, rows, QW), kind),
        tag + "crp": V((2, rows, PW), kind),
        tag + "crq": V((2, rows, QW), kind),
        tag + "owp": V((2, rows, PW), F32),
        tag + "owq": V((2, rows, QW), F32),
        tag + "ps": V((2, rows, PW), kind),
        tag + "qs": V((2, 2, NX, eighth, QW), kind),
        tag + "pr": V((2, 3, quarter, PW), kind),
        tag + "qr": V((3, NX, eighth, QW), kind),
        tag + "p2": V((2, 2, eighth, PW), kind),
        tag + "p2f": V((2, 2, eighth, PW), F32),
        tag + "q2": V((NX, eighth, QW), kind),
        tag + "q2f": V((NX, eighth, QW), F32),
        tag + "pr2": V((3, eighth, PW), kind),
        tag + "qr2": V((3, eighth, QW), kind),
        tag + "f": V((2 * rows, KH), BF) if rows >= 128 else V((16, 16, KH // 2), BF),
    }


def scratch():
    V = pltpu.VMEM
    shapes = {
        "x": V((2, 2 * ROWS, IB), BF),
        "b": V((IB, KB), BF),
        "bin": V((JB, LB), BF),
        "eig": V((KH, LB), BF),
        "ql": V((IB, 128), BF),
        "qr": V((JB, 128), BF),
        "qlt": V((128, IB), BF),
        "y": V((8, 2, 32, JB), BF),
        "qrt": V((128, JB), BF),
        "rs": V((8, 16, 256), F32),
        "rr": V((8, 16, 256), F32),
        "ro": V((8, 16, 256), F32),
        "rzr": V((7, 16, 256), F32),
        "rfin": V((8, 2, 16, 256), BF),
        "ao": V((8, 64, 256), F32),
        "azs": V((8, 64, 256), BF),
        "azr": V((7, 64, 256), BF),
        "ads": V((8, 64, 256), BF),
        "adr": V((8, 64, 256), BF),
        "afin": V((8, 2, 64, 256), BF),
        "rm": V((NQ, 128, LB), BF),
        "lt": V((KH, 128), BF),
        "pq": V((NQ, KH, LB), BF),
        "at": V((2 * ROWS, LB), F32),
        "sv": V((2, NQ, 2 * ROWS, LB), F32),
        "mc": V((2 * ROWS, 128), F32),
        "m": V((TOK, 128), F32),
        "dmp": V((4, 8, 128), F32),
        "dmz": V((7, 8, 128), F32),
        "dmx": V((3, 8, 128), F32),
        "dmy": V((3, 8, 128), F32),
        "dmc": V((8, 128), F32),
        "fcs": V((2, 8, 128), F32),
        "fzr": V((15, 8, 128), F32),
        "fps": V((8, 128), F32),
        "fpr": V((15, 8, 128), F32),
        "fin": V((2, 8, 128), F32),
    }
    shapes.update(plane_scratch("l_", 64, F32))
    shapes.update(plane_scratch("a_", ROWS, BF))
    shapes.update(plane_scratch("b_", ROWS, BF))
    return shapes


N_SEND = 64
N_RECV = 70
NAMES = tuple(scratch())


def kernel(xg, yg, b_hbm, bin_hbm, eig_hbm, ql_hbm, qr_hbm, out_ref, *refs):
    s = dict(zip(NAMES, refs))
    send_sems, recv_sems, local_sems = refs[len(NAMES) :]
    d = lax.axis_index("dp")
    r = lax.axis_index("row")
    c = lax.axis_index("col")
    x = c // 4
    yl = lax.rem(c // 2, 2)
    e = lax.rem(c, 2)

    def dev(dp=None, z=None, xx=None, yy=None, ee=None):
        dp = d if dp is None else dp
        z = r if z is None else z
        xx = x if xx is None else xx
        yy = yl if yy is None else yy
        ee = e if ee is None else ee
        return {"dp": dp, "row": z, "col": xx * 4 + yy * 2 + ee}

    def zp(off):
        return lax.rem(r + off, NZ)

    def xp(off):
        return lax.rem(x + off, NX)

    y_peers = ((1 - d, yl), (1 - d, 1 - yl), (d, 1 - yl))

    started = []
    settled = []
    landings = []
    local_started = []

    def describe(src, dst, device, send_index, landing):
        return pltpu.make_async_remote_copy(
            src_ref=src,
            dst_ref=dst,
            send_sem=send_sems.at[send_index],
            recv_sem=recv_sems.at[landing],
            device_id=device,
            device_id_type=MESH,
        )

    def settle(count):
        while len(settled) < count:
            started[len(settled)].wait_send()
            settled.append(True)

    def start(src, dst, device, landing):
        settle(len(started) - N_SEND + 1)
        copy = describe(src, dst, device, len(started) % N_SEND, landing)
        copy.start()
        started.append(copy)
        return copy

    def send(src, dst, device):
        landings.append(True)
        return start(src, dst, device, len(landings) - 1)

    def together(extent, copies):
        landings.append(True)
        landing = len(landings) - 1
        for src, dst, device in copies:
            start(src, dst, device, landing)
        return [describe(extent, extent, dev(ee=1 - e), 0, landing)]

    def fetch(src, dst):
        copy = pltpu.make_async_copy(src, dst, local_sems.at[len(local_started)])
        copy.start()
        local_started.append(copy)
        return copy

    def got(copies):
        for copy in copies:
            copy.wait_recv()

    def aligned(value, step):
        return pl.multiple_of(value, step)

    get_b = fetch(b_hbm, s["b"])
    get_ql = fetch(ql_hbm, s["ql"])
    get_qr = fetch(qr_hbm, s["qr"])
    get_bin = fetch(bin_hbm, s["bin"])
    get_eig = fetch(eig_hbm.at[pl.ds(aligned(d * KH, 256), KH)], s["eig"])

    def place(rel, part=None):
        position = ORDER.index(rel)
        base = lax.rem(position % 4 + 2 * e, 4) * 64
        if part is None:
            return s["x"].at[position // 4, pl.ds(aligned(base, 64), 64)]
        return s["x"].at[position // 4, pl.ds(aligned(base + part * 32, 32), 32)]

    get_x = fetch(xg, place(0))
    get_y = fetch(yg, s["y"].at[x * 2 + yl, e])

    barrier = pltpu.get_barrier_semaphore()
    peers = [dev(z=zp(off)) for off in range(1, NZ)]
    for off in range(NX):
        for dp, yy in ((d, yl),) + y_peers:
            if off or dp is not d or yy is not yl:
                peers.append(dev(dp=dp, xx=xp(off), yy=yy))
    peers += [dev(z=zp(off), ee=1 - e) for off in range(NZ)]
    for peer in peers:
        pl.semaphore_signal(barrier, inc=1, device_id=peer, device_id_type=MESH)
    partner = dev(ee=1 - e)

    def partial_group(tag, rows, lhs, h, q_group):
        width = QW if q_group else PW
        own, out = (s[tag + "owq"], s[tag + "csq"]) if q_group else (s[tag + "owp"], s[tag + "csp"])
        landing = s[tag + "crq"] if q_group else s[tag + "crp"]
        base = h * KH + (PW if q_group else 0)

        def tile(j, carry):
            columns = pl.ds(aligned(base + j * TILE, 128), TILE)
            part = jnp.dot(lhs[...], s["b"][:, columns], preferred_element_type=F32)
            here = pl.ds(aligned(j * TILE, TILE), TILE)
            own[h, :, here] = part[:rows]
            out[h, :, here] = part[rows:].astype(out.dtype)
            return carry

        lax.fori_loop(0, width // TILE, tile, 0)
        return lambda: send(out.at[h], landing.at[h], partner)

    def chip_sum(tag, rows, h, q_group):
        eighth = rows // 8
        own = s[tag + "owq"] if q_group else s[tag + "owp"]
        landing = s[tag + "crq"] if q_group else s[tag + "crp"]
        out = s[tag + "qs"] if q_group else s[tag + "ps"]

        def chunk(i, carry):
            here = pl.ds(aligned(i * eighth, eighth), eighth)
            total = own[h, here, :] + landing[h, here, :].astype(F32)
            own[h, here, :] = total
            if q_group:
                out[h, lax.rem(i, 2), i // 2] = total.astype(out.dtype)
            else:
                out[h, here, :] = total.astype(out.dtype)
            return carry

        lax.fori_loop(0, 8, chunk, 0)

    def first_p(tag, rows, h, slot_h):
        quarter = rows // 4
        copies = [
            (
                s[tag + "ps"].at[h, pl.ds(aligned(xp(off) * quarter, quarter), quarter)],
                s[tag + "pr"].at[h, off - 1],
                dev(xx=xp(off)),
            )
            for off in range(1, NX)
        ]
        return together(s[tag + "pr"].at[h], copies)

    def first_q(tag, which):
        landing = s[tag + "qr"]
        copies = [
            (s[tag + "qs"].at[dp, yy], landing.at[i], dev(dp=dp, yy=yy))
            for i, (dp, yy) in enumerate(y_peers)
            if i in which
        ]
        return together(landing.at[pl.ds(which[0], len(which))], copies)

    def second_p(tag, rows, h, which):
        eighth, quarter = rows // 8, rows // 4
        for yy in range(2):
            here = pl.ds(aligned(x * quarter + yy * eighth, eighth), eighth)
            total = s[tag + "owp"][h, here, :]
            for i in range(3):
                total += s[tag + "pr"][h, i, yy * eighth : (yy + 1) * eighth, :].astype(F32)
            s[tag + "p2f"][h, yy] = total
            s[tag + "p2"][h, yy] = total.astype(s[tag + "p2"].dtype)
        landing = s[tag + "pr2"]
        copies = [
            (s[tag + "p2"].at[dp, yy], landing.at[i], dev(dp=dp, yy=yy))
            for i, (dp, yy) in enumerate(y_peers)
            if i in which
        ]
        return together(landing.at[pl.ds(which[0], len(which))], copies)

    def second_q(tag, rows):
        eighth, quarter = rows // 8, rows // 4
        for xx in range(NX):
            here = pl.ds(aligned(xx * quarter + yl * eighth, eighth), eighth)
            total = s[tag + "owq"][d, here, :]
            for i in range(3):
                total += s[tag + "qr"][i, xx].astype(F32)
            s[tag + "q2f"][xx] = total
            s[tag + "q2"][xx] = total.astype(s[tag + "q2"].dtype)
        copies = [
            (s[tag + "q2"].at[xp(off)], s[tag + "qr2"].at[off - 1], dev(xx=xp(off)))
            for off in range(1, NX)
        ]
        return together(s[tag + "qr2"], copies)

    def last_sum(tag, rows):
        eighth, quarter = rows // 8, rows // 4
        here = pl.ds(aligned(e * rows + x * quarter + yl * eighth, eighth), eighth)
        p_total = s[tag + "p2f"][d, yl]
        q_total = s[tag + "q2f"][x]
        for i in range(3):
            p_total += s[tag + "pr2"][i].astype(F32)
            q_total += s[tag + "qr2"][i].astype(F32)
        if rows >= 128:
            s[tag + "f"][here, :PW] = p_total.astype(BF)
            s[tag + "f"][here, PW:] = q_total.astype(BF)
            block = s[tag + "f"].at[here]
        else:
            whole = jnp.concatenate([p_total, q_total], axis=1)
            halves = [whole[:, : KH // 2], whole[:, KH // 2 :]]
            s[tag + "f"][e * 8 + x * 2 + yl] = jnp.concatenate(halves, axis=0).astype(BF)
            block = s[tag + "f"].at[e * 8 + x * 2 + yl]
        copies = []
        for off in range(NX):
            for yy in (yl, 1 - yl):
                if off or yy is not yl:
                    copies.append((block, block, dev(xx=xp(off), yy=yy)))
        return together(s[tag + "f"].at[pl.ds(0, 7 * eighth if rows >= 128 else 7)], copies)

    def to_partner(tag, rows):
        count = rows if rows >= 128 else 8
        block = s[tag + "f"].at[pl.ds(aligned(e * count, count), count)]
        return [send(block, block, partner)]

    groups = ((1 - d, True), (1 - d, False), (d, True), (d, False))

    pl.semaphore_wait(barrier, len(peers))

    right, left = dev(z=zp(1)), dev(z=zp(NZ - 1))

    def own_half(part):
        return xg.at[pl.ds(part * 32, 32)]

    z_in = [
        [send(own_half(part), place(-1, part), right), send(own_half(part), place(1, part), left)]
        for part in range(2)
    ]

    def along_z(distance, arrived):
        copies = []
        for part in range(2):
            got(arrived[part])
            copies.append([])
            if distance < 3 or part == 0:
                far = 4 if distance == 3 else -distance - 1
                copies[part].append(send(place(-distance, part), place(far, part), right))
            if distance < 3 or part == 1:
                copies[part].append(send(place(distance, part), place(distance + 1, part), left))
        return copies

    mine = s["y"].at[x * 2 + yl, e]
    y_in = []
    for off in range(NX):
        for yy in (yl, 1 - yl):
            if off or yy is not yl:
                y_in.append((yg, mine, dev(xx=xp(off), yy=yy)))
    y_in = together(s["y"].at[pl.ds(0, 7), 0], y_in)

    def half_columns(half):
        return pl.ds(aligned(half * 256, 256), 256)

    get_ql.wait()
    turned = s["ql"][...].astype(F32).T.astype(BF)
    s["qlt"][:64] = jnp.where(e == 0, turned[:64], turned[64:])
    s["qlt"][64:] = jnp.where(e == 0, turned[64:], turned[:64])
    get_qr.wait()
    s["qrt"][...] = s["qr"][...].astype(F32).T.astype(BF)
    get_bin.wait()
    factor_part = jnp.dot(s["qrt"][...], s["bin"][:, half_columns(1 - d)], preferred_element_type=F32)
    s["rs"][...] = factor_part.reshape(8, 16, 256)
    r_dp = [send(s["rs"], s["rr"], dev(dp=1 - d))]
    factor_part = jnp.dot(s["qrt"][...], s["bin"][:, half_columns(d)], preferred_element_type=F32)
    s["ro"][...] = factor_part.reshape(8, 16, 256)

    get_b.wait()
    l_core = [partial_group("l_", 64, s["qlt"], h, q)() for h, q in groups[:2]]
    z_in = along_z(1, z_in)
    l_core += [partial_group("l_", 64, s["qlt"], h, q)() for h, q in groups[2:]]

    def first_steps(tag, rows, core_copies, i):
        h, q_group = groups[i]
        got([core_copies[i]])
        chip_sum(tag, rows, h, q_group)
        if q_group:
            return first_q(tag, (0, 1) if i == 0 else (2,))
        return first_p(tag, rows, h, i)

    got(y_in)
    get_y.wait()
    y_half = s["y"].at[:, e]
    y_core = [send(y_half, y_half, partner)]

    got(y_core)
    def input_part(half):
        part = jnp.dot(
            s["y"][...].reshape(TOK, JB), s["bin"][:, half_columns(half)], preferred_element_type=F32
        )
        return part.reshape(8, 64, 256)

    s["ads"][...] = input_part(1 - d).astype(BF)
    a_dp = [send(s["ads"], s["adr"], dev(dp=1 - d))]
    s["ao"][...] = input_part(d)

    z_in = along_z(2, z_in)
    get_x.wait()
    l_first = [first_steps("l_", 64, l_core, i) for i in range(4)]

    a_core, a_first_in = [], []
    for i in range(4):
        a_core.append(partial_group("a_", ROWS, s["x"].at[0], *groups[i])())
        if i:
            a_first_in.append(first_steps("a_", ROWS, a_core, i - 1))
        if i == 1:
            z_in = along_z(3, z_in)
    a_first_in.append(first_steps("a_", ROWS, a_core, 3))
    got(a_dp)
    summed = s["ao"][...] + s["adr"][...].astype(F32)
    s["ao"][...] = summed
    s["azs"][...] = summed.astype(BF)
    a_z = together(s["azr"], [(s["azs"].at[zp(off)], s["azr"].at[off - 1], dev(z=zp(off))) for off in range(1, NZ)])

    get_eig.wait()

    def eig_sum(i, total):
        rows = s["eig"][pl.ds(aligned(i * 128, 128), 128), :].astype(F32)
        return total + jnp.sum(rows.reshape(16, 8, LB), axis=0)

    total = lax.fori_loop(0, KH // 128, eig_sum, jnp.zeros((8, LB), F32))
    s["dmp"][0] = total[:, :128] + total[:, 128:256] + total[:, 256:384] + total[:, 384:]
    dm_z = together(s["dmz"], [(s["dmp"].at[0], s["dmz"].at[off - 1], dev(z=zp(off))) for off in range(1, NZ)])

    got(r_dp)
    s["ro"][...] += s["rr"][...]
    r_z = together(s["rzr"], [(s["ro"].at[zp(off)], s["rzr"].at[off - 1], dev(z=zp(off))) for off in range(1, NZ)])

    def second_steps(tag, rows, first):
        got(first[0])
        got(first[2])
        copies = second_q(tag, rows)
        got(first[1])
        copies += second_p(tag, rows, 1 - d, (0, 1))
        got(first[3])
        return copies + second_p(tag, rows, d, (2,))

    l_second = second_steps("l_", 64, l_first)

    got(z_in[0] + z_in[1])
    b_core, b_first_in = [], []
    for i in range(4):
        b_core.append(partial_group("b_", ROWS, s["x"].at[1], *groups[i])())
        if i:
            b_first_in.append(first_steps("b_", ROWS, b_core, i - 1))
    b_first_in.append(first_steps("b_", ROWS, b_core, 3))

    got(dm_z)
    s["dmp"][1] = s["dmp"][0] + jnp.sum(s["dmz"][...], axis=0)
    dm_x = together(s["dmx"], [(s["dmp"].at[1], s["dmx"].at[off - 1], dev(xx=xp(off))) for off in range(1, NX)])

    got(r_z)
    factors = s["ro"][r] + jnp.sum(s["rzr"][...], axis=0)
    s["rfin"][r, d] = factors.astype(BF)
    mine = s["rfin"].at[r, d]
    r_x = [send(mine, mine, dev(dp=1 - d))]

    got(l_second)
    l_f = last_sum("l_", 64)

    a_second = second_steps("a_", ROWS, a_first_in)

    got(dm_x)
    s["dmp"][2] = s["dmp"][1] + jnp.sum(s["dmx"][...], axis=0)
    dm_y = together(
        s["dmy"],
        [(s["dmp"].at[2], s["dmy"].at[i], dev(dp=dp, yy=yy)) for i, (dp, yy) in enumerate(y_peers)],
    )

    got(a_z)
    summed = s["ao"][r]
    for i in range(7):
        summed += s["azr"][i].astype(F32)
    s["afin"][r, d] = summed.astype(BF)
    mine = s["afin"].at[r, d]
    a_x = [send(mine, mine, dev(dp=1 - d))]

    got(r_x)
    mine = s["rfin"].at[r]
    r_f = together(s["rfin"].at[pl.ds(0, 7)], [(mine, mine, dev(z=zp(off))) for off in range(1, NZ)])
    got(l_f)
    l_last = to_partner("l_", 64)

    got(a_second)
    a_out = last_sum("a_", ROWS)

    got(dm_y)
    s["dmp"][3] = s["dmp"][2] + jnp.sum(s["dmy"][...], axis=0)
    dm_c = [send(s["dmp"].at[3], s["dmc"], partner)]
    got(a_x)
    mine = s["afin"].at[r]
    a_f = together(s["afin"].at[pl.ds(0, 7)], [(mine, mine, dev(z=zp(off))) for off in range(1, NZ)])
    b_second = second_steps("b_", ROWS, b_first_in)

    got(dm_c)
    damping = jnp.sum(s["dmp"][3] + s["dmc"][...], keepdims=True) * (DAMP_RATIO / (DG * DA))
    got(l_last)
    for i in range(2):
        left_rows = s["l_f"][...].astype(F32)[:, i * 8 : (i + 1) * 8].reshape(128, KH // 2)
        s["lt"][i * (KH // 2) : (i + 1) * (KH // 2)] = left_rows.T.astype(BF)
    got(r_f)
    for q in range(NQ):
        s["rm"][q] = jnp.zeros((128, LB), BF)
        for g in range(2):
            rows = slice(q * RANK + g * 16, q * RANK + (g + 1) * 16)
            for half in range(2):
                s["rm"][q, rows, half * 256 : (half + 1) * 256] = s["rfin"][q * 2 + g, half]

    def precondition(i, carry):
        rows = pl.ds(aligned(i * 128, 128), 128)
        inverse = 1.0 / (s["eig"][rows, :].astype(F32) + damping)
        left_rows = s["lt"][rows, :]
        for q in range(NQ):
            product = jnp.dot(left_rows, s["rm"][q], preferred_element_type=F32)
            s["pq"][q, rows, :] = (product * inverse).astype(BF)
        return carry

    lax.fori_loop(0, KH // 128, precondition, 0)

    got(b_second)
    b_out = last_sum("b_", ROWS)

    got(a_out)
    a_both = to_partner("a_", ROWS)

    lanes = lax.broadcasted_iota(jnp.int32, (2 * ROWS, 128), 1)
    block_of = lax.broadcasted_iota(jnp.int32, (2 * ROWS, 128), 0) // 64

    def weigh(tag, chunk):
        def one_query(q, carry):
            s["sv"][chunk, q] = jnp.dot(s[tag + "f"][...], s["pq"][q], preferred_element_type=F32)
            return carry

        lax.fori_loop(0, NQ, one_query, 0)

    def score(chunk):
        blocks = [lax.rem(r + ORDER[chunk * 4 + j] + NZ, NZ) for j in range(4)]
        odd = jnp.zeros_like(lanes)
        for j, block in enumerate(blocks):
            odd = jnp.where(block_of == j, lax.rem(block // 2, 2), odd)
            for half in range(2):
                columns = slice(half * 256, (half + 1) * 256)
                s["at"][j * 64 : (j + 1) * 64, columns] = s["afin"][block, half].astype(F32)
        s["mc"][...] = jnp.zeros((2 * ROWS, 128), F32)

        def one_query(q, carry):
            terms = s["sv"][chunk, q] * s["at"][...]
            total = terms[:, :128] + terms[:, 128:256] + terms[:, 256:384] + terms[:, 384:]
            scores = jnp.sum(total, axis=1, keepdims=True)
            s["mc"][...] += jnp.where(lanes == q + 4 * odd, scores, 0.0)
            return carry

        lax.fori_loop(0, NQ, one_query, 0)
        for j, block in enumerate(blocks):
            s["m"][pl.ds(aligned(block * 64, 64), 64), :] = s["mc"][j * 64 : (j + 1) * 64, :]

    got(a_both)
    weigh("a_", 0)
    got(b_out)
    b_both = to_partner("b_", ROWS)
    settle(len(started) - 9)
    got(b_both)
    weigh("b_", 1)
    got(a_f)
    score(0)
    score(1)

    turned = s["m"][...].T[:8]
    for half in range(2):
        base = half * 256
        s["fcs"][half] = turned[:, base : base + 128] + turned[:, base + 128 : base + 256]
    f_z = []
    for off in range(NZ):
        for ee in (e, 1 - e):
            if off or ee is not e:
                f_z.append((s["fcs"].at[ee], s["fzr"].at[len(f_z)], dev(z=zp(off), ee=ee)))
    got(together(s["fzr"], f_z))
    s["fps"][...] = s["fcs"][e] + jnp.sum(s["fzr"][...], axis=0)
    f_plane = []
    for off in range(NX):
        for dp, yy in ((d, yl),) + y_peers:
            if off or dp is not d or yy is not yl:
                f_plane.append((s["fps"], s["fpr"].at[len(f_plane)], dev(dp=dp, xx=xp(off), yy=yy)))
    got(together(s["fpr"], f_plane))
    s["fin"][e] = s["fps"][...] + jnp.sum(s["fpr"][...], axis=0)
    mine = s["fin"].at[e]
    f_last = [send(mine, mine, partner)]
    got(f_last)
    for half in range(2):
        for part in range(2):
            columns = slice((half * 2 + part) * 128, (half * 2 + part + 1) * 128)
            low = s["fin"][half, part * 4 : part * 4 + 2, :]
            high = s["fin"][half, part * 4 + 2 : part * 4 + 4, :]
            out_ref[:, columns] = jnp.where(d == 0, low, high)

    settle(len(started))
    assert len(landings) <= N_RECV


def local(out_grads, layer_inputs, basis_output, basis_input, eigenvalues, query_left, query_right):
    any_space = pl.BlockSpec(memory_space=pl.ANY)
    return pl.pallas_call(
        kernel,
        out_shape=jax.ShapeDtypeStruct((2, TOK), F32),
        in_specs=[any_space] * 7,
        out_specs=pl.BlockSpec(memory_space=pltpu.VMEM),
        scratch_shapes=list(scratch().values())
        + [
            pltpu.SemaphoreType.DMA((N_SEND,)),
            pltpu.SemaphoreType.DMA((N_RECV,)),
            pltpu.SemaphoreType.DMA((8,)),
        ],
        compiler_params=pltpu.CompilerParams(
            collective_id=0, has_side_effects=True, vmem_limit_bytes=60 * 1024 * 1024
        ),
        cost_estimate=pl.CostEstimate(flops=9_000_000_000, bytes_accessed=11_000_000, transcendentals=0),
    )(out_grads, layer_inputs, basis_output, basis_input, eigenvalues, query_left, query_right)


def solution(mesh):
    in_specs = (
        P("row", ("dp", "col")),
        P("col", ("dp", "row")),
        P(("dp", "col"), "row"),
        P(("dp", "row"), "col"),
        P("row", "col"),
        P(("dp", "col"), None),
        P(("dp", "row"), None),
    )
    return jax.shard_map(
        local, mesh=mesh, in_specs=in_specs, out_specs=P("dp", None), check_vma=False
    )
```

```python
import jax
import jax.numpy as jnp
from jax import lax
from jax.experimental import pallas as pl
from jax.experimental.pallas import tpu as pltpu
from jax.sharding import PartitionSpec as P

DG = 28672
DA = 8192
RANK = 32
NQ = 4
TOK = 512
DAMP_RATIO = 0.1

NX = 4
NZ = 8
KB = 3584
KH = KB // 2
IB = 896
LB = 512
JB = 512
PW = 1024
QW = KH - PW
TILE = 256
ROWS = 128
ORDER = (0, -1, 1, -2, 2, -3, 3, 4)

BF = jnp.bfloat16
F32 = jnp.float32
MESH = pl.DeviceIdType.MESH


def plane_scratch(tag, rows, kind):
    eighth, quarter = rows // 8, rows // 4
    V = pltpu.VMEM
    return {
        tag + "csp": V((2, rows, PW), kind),
        tag + "csq": V((2, rows, QW), kind),
        tag + "crp": V((2, rows, PW), kind),
        tag + "crq": V((2, rows, QW), kind),
        tag + "owp": V((2, rows, PW), F32),
        tag + "owq": V((2, rows, QW), F32),
        tag + "ps": V((2, rows, PW), kind),
        tag + "qs": V((2, 2, NX, eighth, QW), kind),
        tag + "pr": V((2, 3, quarter, PW), kind),
        tag + "qr": V((3, NX, eighth, QW), kind),
        tag + "p2": V((2, 2, eighth, PW), kind),
        tag + "p2f": V((2, 2, eighth, PW), F32),
        tag + "q2": V((NX, eighth, QW), kind),
        tag + "q2f": V((NX, eighth, QW), F32),
        tag + "pr2": V((3, eighth, PW), kind),
        tag + "qr2": V((3, eighth, QW), kind),
        tag + "f": V((2 * rows, KH), BF) if rows >= 128 else V((16, 16, KH // 2), BF),
    }


def scratch():
    V = pltpu.VMEM
    shapes = {
        "x": V((2, 2 * ROWS, IB), BF),
        "b": V((IB, KB), BF),
        "bin": V((JB, LB), BF),
        "eig": V((KH, LB), BF),
        "ql": V((IB, 128), BF),
        "qr": V((JB, 128), BF),
        "qlt": V((128, IB), BF),
        "y": V((8, 2, 32, JB), BF),
        "qrt": V((128, JB), BF),
        "rs": V((8, 16, 256), F32),
        "rr": V((8, 16, 256), F32),
        "ro": V((8, 16, 256), F32),
        "rzr": V((7, 16, 256), F32),
        "rfin": V((8, 2, 16, 256), BF),
        "ao": V((8, 64, 256), F32),
        "azs": V((8, 64, 256), BF),
        "azr": V((7, 64, 256), BF),
        "ads": V((8, 64, 256), BF),
        "adr": V((8, 64, 256), BF),
        "afin": V((8, 2, 64, 256), BF),
        "rm": V((NQ, 128, LB), BF),
        "lt": V((KH, 128), BF),
        "pq": V((NQ, KH, LB), BF),
        "at": V((2 * ROWS, LB), F32),
        "sv": V((2, NQ, 2 * ROWS, LB), F32),
        "mc": V((2 * ROWS, 128), F32),
        "m": V((TOK, 128), F32),
        "dmp": V((4, 8, 128), F32),
        "dmz": V((7, 8, 128), F32),
        "dmx": V((3, 8, 128), F32),
        "dmy": V((3, 8, 128), F32),
        "dmc": V((8, 128), F32),
        "fcs": V((2, 8, 128), F32),
        "fzr": V((15, 8, 128), F32),
        "fps": V((8, 128), F32),
        "fpr": V((15, 8, 128), F32),
        "fin": V((2, 8, 128), F32),
    }
    shapes.update(plane_scratch("l_", 64, F32))
    shapes.update(plane_scratch("a_", ROWS, BF))
    shapes.update(plane_scratch("b_", ROWS, BF))
    return shapes


N_SEND = 64
N_RECV = 70
NAMES = tuple(scratch())


def kernel(xg, yg, b_hbm, bin_hbm, eig_hbm, ql_hbm, qr_hbm, out_ref, *refs):
    s = dict(zip(NAMES, refs))
    send_sems, recv_sems, local_sems = refs[len(NAMES) :]
    d = lax.axis_index("dp")
    r = lax.axis_index("row")
    c = lax.axis_index("col")
    x = c // 4
    yl = lax.rem(c // 2, 2)
    e = lax.rem(c, 2)

    def dev(dp=None, z=None, xx=None, yy=None, ee=None):
        dp = d if dp is None else dp
        z = r if z is None else z
        xx = x if xx is None else xx
        yy = yl if yy is None else yy
        ee = e if ee is None else ee
        return {"dp": dp, "row": z, "col": xx * 4 + yy * 2 + ee}

    def zp(off):
        return lax.rem(r + off, NZ)

    def xp(off):
        return lax.rem(x + off, NX)

    y_peers = ((1 - d, yl), (1 - d, 1 - yl), (d, 1 - yl))

    started = []
    settled = []
    landings = []
    local_started = []

    def describe(src, dst, device, send_index, landing):
        return pltpu.make_async_remote_copy(
            src_ref=src,
            dst_ref=dst,
            send_sem=send_sems.at[send_index],
            recv_sem=recv_sems.at[landing],
            device_id=device,
            device_id_type=MESH,
        )

    def settle(count):
        while len(settled) < count:
            started[len(settled)].wait_send()
            settled.append(True)

    def start(src, dst, device, landing):
        settle(len(started) - N_SEND + 1)
        copy = describe(src, dst, device, len(started) % N_SEND, landing)
        copy.start()
        started.append(copy)
        return copy

    def send(src, dst, device):
        landings.append(True)
        return start(src, dst, device, len(landings) - 1)

    def together(extent, copies):
        landings.append(True)
        landing = len(landings) - 1
        for src, dst, device in copies:
            start(src, dst, device, landing)
        return [describe(extent, extent, dev(ee=1 - e), 0, landing)]

    def fetch(src, dst):
        copy = pltpu.make_async_copy(src, dst, local_sems.at[len(local_started)])
        copy.start()
        local_started.append(copy)
        return copy

    def got(copies):
        for copy in copies:
            copy.wait_recv()

    def aligned(value, step):
        return pl.multiple_of(value, step)

    get_b = fetch(b_hbm, s["b"])
    get_ql = fetch(ql_hbm, s["ql"])
    get_qr = fetch(qr_hbm, s["qr"])
    get_bin = fetch(bin_hbm, s["bin"])
    get_eig = fetch(eig_hbm.at[pl.ds(aligned(d * KH, 256), KH)], s["eig"])

    def place(rel, part=None):
        position = ORDER.index(rel)
        base = lax.rem(position % 4 + 2 * e, 4) * 64
        if part is None:
            return s["x"].at[position // 4, pl.ds(aligned(base, 64), 64)]
        return s["x"].at[position // 4, pl.ds(aligned(base + part * 32, 32), 32)]

    get_x = fetch(xg, place(0))
    get_y = fetch(yg, s["y"].at[x * 2 + yl, e])

    barrier = pltpu.get_barrier_semaphore()
    peers = [dev(z=zp(off)) for off in range(1, NZ)]
    for off in range(NX):
        for dp, yy in ((d, yl),) + y_peers:
            if off or dp is not d or yy is not yl:
                peers.append(dev(dp=dp, xx=xp(off), yy=yy))
    peers += [dev(z=zp(off), ee=1 - e) for off in range(NZ)]
    for peer in peers:
        pl.semaphore_signal(barrier, inc=1, device_id=peer, device_id_type=MESH)
    partner = dev(ee=1 - e)

    def partial_group(tag, rows, lhs, h, q_group):
        width = QW if q_group else PW
        own, out = (s[tag + "owq"], s[tag + "csq"]) if q_group else (s[tag + "owp"], s[tag + "csp"])
        landing = s[tag + "crq"] if q_group else s[tag + "crp"]
        base = h * KH + (PW if q_group else 0)

        def tile(j, carry):
            columns = pl.ds(aligned(base + j * TILE, 128), TILE)
            part = jnp.dot(lhs[...], s["b"][:, columns], preferred_element_type=F32)
            here = pl.ds(aligned(j * TILE, TILE), TILE)
            own[h, :, here] = part[:rows]
            out[h, :, here] = part[rows:].astype(out.dtype)
            return carry

        lax.fori_loop(0, width // TILE, tile, 0)
        return lambda: send(out.at[h], landing.at[h], partner)

    def chip_sum(tag, rows, h, q_group):
        eighth = rows // 8
        own = s[tag + "owq"] if q_group else s[tag + "owp"]
        landing = s[tag + "crq"] if q_group else s[tag + "crp"]
        out = s[tag + "qs"] if q_group else s[tag + "ps"]

        def chunk(i, carry):
            here = pl.ds(aligned(i * eighth, eighth), eighth)
            total = own[h, here, :] + landing[h, here, :].astype(F32)
            own[h, here, :] = total
            if q_group:
                out[h, lax.rem(i, 2), i // 2] = total.astype(out.dtype)
            else:
                out[h, here, :] = total.astype(out.dtype)
            return carry

        lax.fori_loop(0, 8, chunk, 0)

    def first_p(tag, rows, h, slot_h):
        quarter = rows // 4
        copies = [
            (
                s[tag + "ps"].at[h, pl.ds(aligned(xp(off) * quarter, quarter), quarter)],
                s[tag + "pr"].at[h, off - 1],
                dev(xx=xp(off)),
            )
            for off in range(1, NX)
        ]
        return together(s[tag + "pr"].at[h], copies)

    def first_q(tag, which):
        landing = s[tag + "qr"]
        copies = [
            (s[tag + "qs"].at[dp, yy], landing.at[i], dev(dp=dp, yy=yy))
            for i, (dp, yy) in enumerate(y_peers)
            if i in which
        ]
        return together(landing.at[pl.ds(which[0], len(which))], copies)

    def second_p(tag, rows, h, which):
        eighth, quarter = rows // 8, rows // 4
        for yy in range(2):
            here = pl.ds(aligned(x * quarter + yy * eighth, eighth), eighth)
            total = s[tag + "owp"][h, here, :]
            for i in range(3):
                total += s[tag + "pr"][h, i, yy * eighth : (yy + 1) * eighth, :].astype(F32)
            s[tag + "p2f"][h, yy] = total
            s[tag + "p2"][h, yy] = total.astype(s[tag + "p2"].dtype)
        landing = s[tag + "pr2"]
        copies = [
            (s[tag + "p2"].at[dp, yy], landing.at[i], dev(dp=dp, yy=yy))
            for i, (dp, yy) in enumerate(y_peers)
            if i in which
        ]
        return together(landing.at[pl.ds(which[0], len(which))], copies)

    def second_q(tag, rows):
        eighth, quarter = rows // 8, rows // 4
        for xx in range(NX):
            here = pl.ds(aligned(xx * quarter + yl * eighth, eighth), eighth)
            total = s[tag + "owq"][d, here, :]
            for i in range(3):
                total += s[tag + "qr"][i, xx].astype(F32)
            s[tag + "q2f"][xx] = total
            s[tag + "q2"][xx] = total.astype(s[tag + "q2"].dtype)
        copies = [
            (s[tag + "q2"].at[xp(off)], s[tag + "qr2"].at[off - 1], dev(xx=xp(off)))
            for off in range(1, NX)
        ]
        return together(s[tag + "qr2"], copies)

    def last_sum(tag, rows):
        eighth, quarter = rows // 8, rows // 4
        here = pl.ds(aligned(e * rows + x * quarter + yl * eighth, eighth), eighth)
        p_total = s[tag + "p2f"][d, yl]
        q_total = s[tag + "q2f"][x]
        for i in range(3):
            p_total += s[tag + "pr2"][i].astype(F32)
            q_total += s[tag + "qr2"][i].astype(F32)
        if rows >= 128:
            s[tag + "f"][here, :PW] = p_total.astype(BF)
            s[tag + "f"][here, PW:] = q_total.astype(BF)
            block = s[tag + "f"].at[here]
        else:
            whole = jnp.concatenate([p_total, q_total], axis=1)
            halves = [whole[:, : KH // 2], whole[:, KH // 2 :]]
            s[tag + "f"][e * 8 + x * 2 + yl] = jnp.concatenate(halves, axis=0).astype(BF)
            block = s[tag + "f"].at[e * 8 + x * 2 + yl]
        copies = []
        for off in range(NX):
            for yy in (yl, 1 - yl):
                if off or yy is not yl:
                    copies.append((block, block, dev(xx=xp(off), yy=yy)))
        return together(s[tag + "f"].at[pl.ds(0, 7 * eighth if rows >= 128 else 7)], copies)

    def to_partner(tag, rows):
        count = rows if rows >= 128 else 8
        block = s[tag + "f"].at[pl.ds(aligned(e * count, count), count)]
        return [send(block, block, partner)]

    groups = ((1 - d, True), (1 - d, False), (d, True), (d, False))

    pl.semaphore_wait(barrier, len(peers))

    right, left = dev(z=zp(1)), dev(z=zp(NZ - 1))

    def own_half(part):
        return xg.at[pl.ds(part * 32, 32)]

    z_in = [
        [send(own_half(part), place(-1, part), right), send(own_half(part), place(1, part), left)]
        for part in range(2)
    ]

    def along_z(distance, arrived):
        copies = []
        for part in range(2):
            got(arrived[part])
            copies.append([])
            if distance < 3 or part == 0:
                far = 4 if distance == 3 else -distance - 1
                copies[part].append(send(place(-distance, part), place(far, part), right))
            if distance < 3 or part == 1:
                copies[part].append(send(place(distance, part), place(distance + 1, part), left))
        return copies

    mine = s["y"].at[x * 2 + yl, e]
    y_in = []
    for off in range(NX):
        for yy in (yl, 1 - yl):
            if off or yy is not yl:
                y_in.append((yg, mine, dev(xx=xp(off), yy=yy)))
    y_in = together(s["y"].at[pl.ds(0, 7), 0], y_in)

    def half_columns(half):
        return pl.ds(aligned(half * 256, 256), 256)

    get_ql.wait()
    turned = s["ql"][...].astype(F32).T.astype(BF)
    s["qlt"][:64] = jnp.where(e == 0, turned[:64], turned[64:])
    s["qlt"][64:] = jnp.where(e == 0, turned[64:], turned[:64])
    get_qr.wait()
    s["qrt"][...] = s["qr"][...].astype(F32).T.astype(BF)
    get_bin.wait()
    factor_part = jnp.dot(s["qrt"][...], s["bin"][:, half_columns(1 - d)], preferred_element_type=F32)
    s["rs"][...] = factor_part.reshape(8, 16, 256)
    r_dp = [send(s["rs"], s["rr"], dev(dp=1 - d))]
    factor_part = jnp.dot(s["qrt"][...], s["bin"][:, half_columns(d)], preferred_element_type=F32)
    s["ro"][...] = factor_part.reshape(8, 16, 256)

    get_b.wait()
    l_core = [partial_group("l_", 64, s["qlt"], h, q)() for h, q in groups[:2]]
    z_in = along_z(1, z_in)
    l_core += [partial_group("l_", 64, s["qlt"], h, q)() for h, q in groups[2:]]

    def first_steps(tag, rows, core_copies, i):
        h, q_group = groups[i]
        got([core_copies[i]])
        chip_sum(tag, rows, h, q_group)
        if q_group:
            return first_q(tag, (0, 1) if i == 0 else (2,))
        return first_p(tag, rows, h, i)

    got(y_in)
    get_y.wait()
    y_half = s["y"].at[:, e]
    y_core = [send(y_half, y_half, partner)]

    got(y_core)
    def input_part(half):
        part = jnp.dot(
            s["y"][...].reshape(TOK, JB), s["bin"][:, half_columns(half)], preferred_element_type=F32
        )
        return part.reshape(8, 64, 256)

    s["ads"][...] = input_part(1 - d).astype(BF)
    a_dp = [send(s["ads"], s["adr"], dev(dp=1 - d))]
    s["ao"][...] = input_part(d)

    get_eig.wait()

    def eig_sum(i, total):
        rows = s["eig"][pl.ds(aligned(i * 128, 128), 128), :].astype(F32)
        return total + jnp.sum(rows.reshape(16, 8, LB), axis=0)

    total = lax.fori_loop(0, KH // 128, eig_sum, jnp.zeros((8, LB), F32))
    s["dmp"][0] = total[:, :128] + total[:, 128:256] + total[:, 256:384] + total[:, 384:]
    dm_z = together(s["dmz"], [(s["dmp"].at[0], s["dmz"].at[off - 1], dev(z=zp(off))) for off in range(1, NZ)])

    z_in = along_z(2, z_in)
    get_x.wait()
    l_first = [first_steps("l_", 64, l_core, i) for i in range(4)]

    a_core, a_first_in = [], []
    for i in range(4):
        a_core.append(partial_group("a_", ROWS, s["x"].at[0], *groups[i])())
        if i:
            a_first_in.append(first_steps("a_", ROWS, a_core, i - 1))
        if i == 1:
            z_in = along_z(3, z_in)
            got(r_dp)
            s["ro"][...] += s["rr"][...]
            r_z = together(s["rzr"], [(s["ro"].at[zp(off)], s["rzr"].at[off - 1], dev(z=zp(off))) for off in range(1, NZ)])
    a_first_in.append(first_steps("a_", ROWS, a_core, 3))
    got(a_dp)
    summed = s["ao"][...] + s["adr"][...].astype(F32)
    s["ao"][...] = summed
    s["azs"][...] = summed.astype(BF)
    a_z = together(s["azr"], [(s["azs"].at[zp(off)], s["azr"].at[off - 1], dev(z=zp(off))) for off in range(1, NZ)])

    def second_steps(tag, rows, first):
        got(first[0])
        got(first[2])
        copies = second_q(tag, rows)
        got(first[1])
        copies += second_p(tag, rows, 1 - d, (0, 1))
        got(first[3])
        return copies + second_p(tag, rows, d, (2,))

    got(z_in[0] + z_in[1])
    b_core, b_first_in = [], []
    for i in range(4):
        b_core.append(partial_group("b_", ROWS, s["x"].at[1], *groups[i])())
        if i:
            b_first_in.append(first_steps("b_", ROWS, b_core, i - 1))
    b_first_in.append(first_steps("b_", ROWS, b_core, 3))

    a_second = second_steps("a_", ROWS, a_first_in)

    got(dm_z)
    s["dmp"][1] = s["dmp"][0] + jnp.sum(s["dmz"][...], axis=0)
    dm_x = together(s["dmx"], [(s["dmp"].at[1], s["dmx"].at[off - 1], dev(xx=xp(off))) for off in range(1, NX)])

    got(r_z)
    factors = s["ro"][r] + jnp.sum(s["rzr"][...], axis=0)
    s["rfin"][r, d] = factors.astype(BF)
    mine = s["rfin"].at[r, d]
    r_x = [send(mine, mine, dev(dp=1 - d))]

    l_second = second_steps("l_", 64, l_first)

    got(a_z)
    summed = s["ao"][r]
    for i in range(7):
        summed += s["azr"][i].astype(F32)
    s["afin"][r, d] = summed.astype(BF)
    mine = s["afin"].at[r, d]
    a_x = [send(mine, mine, dev(dp=1 - d))]

    got(r_x)
    mine = s["rfin"].at[r]
    r_f = together(s["rfin"].at[pl.ds(0, 7)], [(mine, mine, dev(z=zp(off))) for off in range(1, NZ)])

    got(dm_x)
    s["dmp"][2] = s["dmp"][1] + jnp.sum(s["dmx"][...], axis=0)
    dm_y = together(
        s["dmy"],
        [(s["dmp"].at[2], s["dmy"].at[i], dev(dp=dp, yy=yy)) for i, (dp, yy) in enumerate(y_peers)],
    )

    got(l_second)
    l_f = last_sum("l_", 64)

    got(a_second)
    a_out = last_sum("a_", ROWS)

    got(a_x)
    mine = s["afin"].at[r]
    a_f = together(s["afin"].at[pl.ds(0, 7)], [(mine, mine, dev(z=zp(off))) for off in range(1, NZ)])
    got(dm_y)
    s["dmp"][3] = s["dmp"][2] + jnp.sum(s["dmy"][...], axis=0)
    dm_c = [send(s["dmp"].at[3], s["dmc"], partner)]
    b_second = second_steps("b_", ROWS, b_first_in)

    got(l_f)
    l_last = to_partner("l_", 64)
    got(dm_c)
    damping = jnp.sum(s["dmp"][3] + s["dmc"][...], keepdims=True) * (DAMP_RATIO / (DG * DA))
    got(l_last)
    for i in range(2):
        left_rows = s["l_f"][...].astype(F32)[:, i * 8 : (i + 1) * 8].reshape(128, KH // 2)
        s["lt"][i * (KH // 2) : (i + 1) * (KH // 2)] = left_rows.T.astype(BF)
    got(r_f)
    for q in range(NQ):
        s["rm"][q] = jnp.zeros((128, LB), BF)
        for g in range(2):
            rows = slice(q * RANK + g * 16, q * RANK + (g + 1) * 16)
            for half in range(2):
                s["rm"][q, rows, half * 256 : (half + 1) * 256] = s["rfin"][q * 2 + g, half]

    def precondition(i, carry):
        rows = pl.ds(aligned(i * 128, 128), 128)
        inverse = 1.0 / (s["eig"][rows, :].astype(F32) + damping)
        left_rows = s["lt"][rows, :]
        for q in range(NQ):
            product = jnp.dot(left_rows, s["rm"][q], preferred_element_type=F32)
            s["pq"][q, rows, :] = (product * inverse).astype(BF)
        return carry

    lax.fori_loop(0, KH // 128, precondition, 0)

    got(b_second)
    b_out = last_sum("b_", ROWS)

    got(a_out)
    a_both = to_partner("a_", ROWS)

    lanes = lax.broadcasted_iota(jnp.int32, (2 * ROWS, 128), 1)
    block_of = lax.broadcasted_iota(jnp.int32, (2 * ROWS, 128), 0) // 64

    def weigh(tag, chunk):
        def one_query(q, carry):
            s["sv"][chunk, q] = jnp.dot(s[tag + "f"][...], s["pq"][q], preferred_element_type=F32)
            return carry

        lax.fori_loop(0, NQ, one_query, 0)

    def score(chunk):
        blocks = [lax.rem(r + ORDER[chunk * 4 + j] + NZ, NZ) for j in range(4)]
        odd = jnp.zeros_like(lanes)
        for j, block in enumerate(blocks):
            odd = jnp.where(block_of == j, lax.rem(block // 2, 2), odd)
            for half in range(2):
                columns = slice(half * 256, (half + 1) * 256)
                s["at"][j * 64 : (j + 1) * 64, columns] = s["afin"][block, half].astype(F32)
        s["mc"][...] = jnp.zeros((2 * ROWS, 128), F32)

        def one_query(q, carry):
            terms = s["sv"][chunk, q] * s["at"][...]
            total = terms[:, :128] + terms[:, 128:256] + terms[:, 256:384] + terms[:, 384:]
            scores = jnp.sum(total, axis=1, keepdims=True)
            s["mc"][...] += jnp.where(lanes == q + 4 * odd, scores, 0.0)
            return carry

        lax.fori_loop(0, NQ, one_query, 0)
        for j, block in enumerate(blocks):
            s["m"][pl.ds(aligned(block * 64, 64), 64), :] = s["mc"][j * 64 : (j + 1) * 64, :]

    got(a_both)
    weigh("a_", 0)
    got(b_out)
    b_both = to_partner("b_", ROWS)
    settle(len(started) - 9)
    got(b_both)
    weigh("b_", 1)
    got(a_f)
    score(0)
    score(1)

    turned = s["m"][...].T[:8]
    for half in range(2):
        base = half * 256
        s["fcs"][half] = turned[:, base : base + 128] + turned[:, base + 128 : base + 256]
    f_z = []
    for off in range(NZ):
        for ee in (e, 1 - e):
            if off or ee is not e:
                f_z.append((s["fcs"].at[ee], s["fzr"].at[len(f_z)], dev(z=zp(off), ee=ee)))
    got(together(s["fzr"], f_z))
    s["fps"][...] = s["fcs"][e] + jnp.sum(s["fzr"][...], axis=0)
    f_plane = []
    for off in range(NX):
        for dp, yy in ((d, yl),) + y_peers:
            if off or dp is not d or yy is not yl:
                f_plane.append((s["fps"], s["fpr"].at[len(f_plane)], dev(dp=dp, xx=xp(off), yy=yy)))
    got(together(s["fpr"], f_plane))
    s["fin"][e] = s["fps"][...] + jnp.sum(s["fpr"][...], axis=0)
    mine = s["fin"].at[e]
    f_last = [send(mine, mine, partner)]
    got(f_last)
    for half in range(2):
        for part in range(2):
            columns = slice((half * 2 + part) * 128, (half * 2 + part + 1) * 128)
            low = s["fin"][half, part * 4 : part * 4 + 2, :]
            high = s["fin"][half, part * 4 + 2 : part * 4 + 4, :]
            out_ref[:, columns] = jnp.where(d == 0, low, high)

    settle(len(started))
    assert len(landings) <= N_RECV


def local(out_grads, layer_inputs, basis_output, basis_input, eigenvalues, query_left, query_right):
    any_space = pl.BlockSpec(memory_space=pl.ANY)
    return pl.pallas_call(
        kernel,
        out_shape=jax.ShapeDtypeStruct((2, TOK), F32),
        in_specs=[any_space] * 7,
        out_specs=pl.BlockSpec(memory_space=pltpu.VMEM),
        scratch_shapes=list(scratch().values())
        + [
            pltpu.SemaphoreType.DMA((N_SEND,)),
            pltpu.SemaphoreType.DMA((N_RECV,)),
            pltpu.SemaphoreType.DMA((8,)),
        ],
        compiler_params=pltpu.CompilerParams(
            collective_id=0, has_side_effects=True, vmem_limit_bytes=60 * 1024 * 1024
        ),
        cost_estimate=pl.CostEstimate(flops=9_000_000_000, bytes_accessed=11_000_000, transcendentals=0),
    )(out_grads, layer_inputs, basis_output, basis_input, eigenvalues, query_left, query_right)


def solution(mesh):
    in_specs = (
        P("row", ("dp", "col")),
        P("col", ("dp", "row")),
        P(("dp", "col"), "row"),
        P(("dp", "row"), "col"),
        P("row", "col"),
        P(("dp", "col"), None),
        P(("dp", "row"), None),
    )
    return jax.shard_map(
        local, mesh=mesh, in_specs=in_specs, out_specs=P("dp", None), check_vma=False
    )
```
